512 devices in a mesh: dp: 8 (over x, core), expert: 64 (over y, z).
Axes of the slice: x: 4, y: 4, z: 16, core: 2. Of those that a mesh axis runs over, the one named last changes fastest.
Arguments:
- tokens: bfloat16 [8192, 3584], P(('dp', 'expert')), may hold values from -6 to 6
- cotangent: bfloat16 [8192, 3584], P(('dp', 'expert')), may hold values from -6 to 6
- expert_ids: int32 [8192, 2], P(('dp', 'expert')), may hold values from 0 to 7, all different within a row; in each aligned block of 16 rows (0 to 15, 16 to 31, ...) at most 8 rows name the same one
- gates: bfloat16 [8192, 2], P(('dp', 'expert')), may hold values from 0.049804688 to 1
- w_gate: bfloat16 [64, 3584, 128], P('expert', 'dp'), may hold values from -0.09375 to 0.09375
- w_up: bfloat16 [64, 3584, 128], P('expert', 'dp'), may hold values from -0.09375 to 0.09375
- w_down_t: bfloat16 [64, 3584, 128], P('expert', 'dp'), may hold values from -0.1875 to 0.1875
Outputs:
- grad_tokens: bfloat16 [8192, 3584], P(('dp', 'expert'))
- grad_gates: float32 [8192, 2], P(('dp', 'expert'))
- grad_w_gate: bfloat16 [64, 3584, 128], P('expert', 'dp')
- grad_w_up: bfloat16 [64, 3584, 128], P('expert', 'dp')
- grad_w_down_t: bfloat16 [64, 3584, 128], P('expert', 'dp')
The draws below stay inside these ranges and needn't reach their ends.
Inputs may be any that keep to these rules, and one draw needn't show every extreme that they name: `expert_ids`: each row names 2 different experts; among the 16 rows of one device no expert is named more than 8 times, a bound that some block reaches.
All inputs are finite; a program needn't handle non-finite values.
Results may differ from the reference program's by a relative error of at most 0.02.
Values may be sent and summed in bfloat16 or wider, within the bound.
A program may use at most 64 MiB of HBM per device.

```python
import math
import jax
import jax.numpy as jnp
import numpy as np
from jax import lax

D = 3584
FF = 1024
TOK_DEV = 16
EXPERTS = 8
TOP = 2
FFH = 128
CAP = 8
SLICES = 64
TOKENS = 8192
N_DP = 8
N_EXPERT = 64


def block_levels(rng, extent, pieces, least, high):
    def one(position, parts):
        draws = jax.random.uniform(jax.random.fold_in(jax.random.fold_in(rng, 6), position), (parts,), jnp.float32, least / len(pieces), high / len(pieces))
        return jnp.repeat(jnp.exp(draws), extent[position] // parts).reshape((-1,) + (1,) * (len(extent) - position - 1))

    level = one(*pieces[0])
    for cut in pieces[1:]:
        level = level * one(*cut)
    return level


def shared_out(key, own, number, rows, amount, top, most, lean):
    ranking = jax.random.permutation(key, amount)
    heavy_load, usual = load_shares(amount, rows * top, most, lean, True), load_shares(amount, rows * top, most, lean, False)
    places = jnp.arange(amount)

    def named(lengths, rotation):
        used = int((lengths > 0).sum())
        fixed = max(1, used // 4)
        passed = fixed + (places - fixed + rotation * (used - fixed)) % max(1, amount - fixed)
        return jnp.zeros((amount,), jnp.int32).at[ranking[jnp.where(places < fixed, places, passed)]].set(jnp.asarray(lengths, jnp.int32))

    lengths = jnp.where(number % 4 == 0, named(heavy_load, number // 4), named(usual, number - number // 4 - 1))
    mixed = jax.random.permutation(jax.random.fold_in(own, 3), amount)
    donor, taker = mixed[0:amount // 2 * 2:2], mixed[1:amount // 2 * 2:2]
    slack = jnp.minimum(lengths[donor] - 1, most - lengths[taker]) // 2
    slack = jnp.where((donor == ranking[0]) | (taker == ranking[0]) | (lengths[taker] == 0), 0, jnp.maximum(slack, 0))
    passed = jax.random.randint(jax.random.fold_in(own, 4), (amount // 2,), 0, 1 << 20) % (slack + 1)
    lengths = lengths.at[donor].add(-passed).at[taker].add(passed)
    items = jnp.searchsorted(jnp.cumsum(lengths), jnp.arange(rows * top), side="right").astype(jnp.int32)
    grid = items.reshape(top, rows).T
    grid = grid[jax.random.permutation(jax.random.fold_in(own, 1), rows)]
    rotation = jax.random.randint(jax.random.fold_in(own, 2), (rows, 1), 0, top)
    return jnp.take_along_axis(grid, (jnp.arange(top)[None, :] + rotation) % top, axis=1)


def load_shares(number_of, total, most, lean, full):
    weights = [(1 << 20) // math.isqrt(rank ** lean) + 1 for rank in range(1, number_of + 1)]
    largest = most if full else min(most, max(-(-total // number_of), total * weights[0] // sum(weights)))
    least = 1 if total - largest >= number_of - 1 else 0
    given, surplus = [largest] + [least] * (number_of - 1), total - largest - least * (number_of - 1)
    while surplus > 0:
        candidates = [i for i in range(1, number_of) if given[i] < largest] or [i for i in range(1, number_of) if given[i] < most]
        mass, budget = sum([weights[i] for i in candidates]), surplus
        for i in candidates:
            more = min(most - given[i], max(1, budget * weights[i] // mass), surplus)
            given[i] = given[i] + more
            surplus = surplus - more
    return np.array(given)


def centred(rng, extent, scale, most, shards=(), kind=jnp.bfloat16):
    array = scale * jax.random.normal(rng, extent, jnp.float32)
    if shards:
        array = array * block_levels(rng, extent, shards, -0.22, 0.18)
    return jnp.clip(array, -most, most).astype(kind)


def setup_inputs(seed: int = 0) -> dict:
    seeds = jax.random.split(jax.random.key(seed), 8)
    tokens = centred(seeds[0], (TOKENS, D), 1.0, 6.0, ((0, 512),))
    cotangent = centred(seeds[1], (TOKENS, D), 1.0, 6.0, ((0, 512),))
    expert_ids_keys = jax.random.split(jax.random.fold_in(seeds[2], 1), TOKENS // TOK_DEV)
    expert_ids_turns = jax.random.permutation(jax.random.fold_in(seeds[2], 3), TOKENS // TOK_DEV)
    expert_ids = jax.vmap(lambda own, number: shared_out(jax.random.fold_in(seeds[2], 2), own, number, TOK_DEV, EXPERTS, TOP, CAP, 1))(expert_ids_keys, expert_ids_turns).reshape((TOKENS, TOP))
    gates = jnp.clip(jnp.exp(math.log(1.0) - 2.9996462 * jax.random.uniform(seeds[3], (TOKENS, TOP), jnp.float32) ** block_levels(seeds[3], (TOKENS, TOP), ((0, 512),), -0.2, 0.2)), 0.049804688, 1.0).astype(jnp.bfloat16)
    w_gate = centred(seeds[4], (SLICES, D, FFH), D ** -0.5, 0.09375, ((0, 64), (1, 8)))
    w_up = centred(seeds[5], (SLICES, D, FFH), D ** -0.5, 0.09375, ((0, 64), (1, 8)))
    w_down_t = centred(seeds[6], (SLICES, D, FFH), FF ** -0.5, 0.1875, ((0, 64), (1, 8)))
    return dict(tokens=tokens, cotangent=cotangent, expert_ids=expert_ids, gates=gates, w_gate=w_gate, w_up=w_up, w_down_t=w_down_t)


def slice_work(x_sel, dy_sel, p_sel, wg1, wu1, wd1):
    pre_gate = jnp.dot(x_sel, wg1, preferred_element_type=jnp.float32)
    pre_up = jnp.dot(x_sel, wu1, preferred_element_type=jnp.float32)
    back = jnp.dot(dy_sel, wd1, preferred_element_type=jnp.float32)
    sig = jax.nn.sigmoid(pre_gate)
    silu = pre_gate * sig
    hidden = (silu * pre_up).astype(jnp.bfloat16)
    weight = p_sel.astype(jnp.float32)[:, None]
    d_hidden = weight * back
    part_gate = jnp.sum(hidden.astype(jnp.float32) * back, axis=1).astype(jnp.bfloat16)
    d_gate = (d_hidden * pre_up * sig * (1.0 + pre_gate * (1.0 - sig))).astype(jnp.bfloat16)
    d_up = (d_hidden * silu).astype(jnp.bfloat16)
    scaled = (weight * dy_sel.astype(jnp.float32)).astype(jnp.bfloat16)
    part_tokens = (jnp.dot(d_gate, wg1.T, preferred_element_type=jnp.float32)
                   + jnp.dot(d_up, wu1.T, preferred_element_type=jnp.float32)).astype(jnp.bfloat16)
    g_gate = jnp.dot(x_sel.T, d_gate, preferred_element_type=jnp.float32).astype(jnp.bfloat16)
    g_up = jnp.dot(x_sel.T, d_up, preferred_element_type=jnp.float32).astype(jnp.bfloat16)
    g_down = jnp.dot(scaled.T, hidden, preferred_element_type=jnp.float32).astype(jnp.bfloat16)
    return part_tokens, part_gate, g_gate, g_up, g_down


def reference(tokens, cotangent, expert_ids, gates, w_gate, w_up, w_down_t):
    group = N_EXPERT // EXPERTS
    ffh = FF // group
    block = TOK_DEV * N_EXPERT
    limit = N_EXPERT * CAP
    xb = tokens.reshape(N_DP, block, D)
    yb = cotangent.reshape(N_DP, block, D)
    ib = expert_ids.reshape(N_DP, block, TOP)
    gb = gates.reshape(N_DP, block, TOP)
    wg = w_gate.reshape(EXPERTS, group, D, ffh)
    wu = w_up.reshape(EXPERTS, group, D, ffh)
    wd = w_down_t.reshape(EXPERTS, group, D, ffh)
    zero_row = jnp.zeros((1, D), jnp.bfloat16)

    def step(index, carry):
        acc_x, acc_p, acc_g, acc_u, acc_d = carry
        expert = index // N_DP
        row = index % N_DP
        x = lax.dynamic_index_in_dim(xb, row, 0, keepdims=False)
        dy = lax.dynamic_index_in_dim(yb, row, 0, keepdims=False)
        ids = lax.dynamic_index_in_dim(ib, row, 0, keepdims=False)
        gts = lax.dynamic_index_in_dim(gb, row, 0, keepdims=False)
        hit = ids == expert
        member = jnp.any(hit, axis=1)
        prob = jnp.sum(jnp.where(hit, gts.astype(jnp.float32), jnp.float32(0.0)), axis=1)
        pos = jnp.cumsum(member.astype(jnp.int32)) - 1
        target = jnp.where(member, pos, limit).astype(jnp.int32)
        order = jnp.full((limit,), block, jnp.int32).at[target].set(jnp.arange(block, dtype=jnp.int32), mode="drop")
        x_sel = jnp.concatenate([x, zero_row], axis=0)[order]
        dy_sel = jnp.concatenate([dy, zero_row], axis=0)[order]
        p_sel = jnp.concatenate([prob, jnp.zeros((1,), jnp.float32)])[order].astype(jnp.bfloat16)
        wg_e = lax.dynamic_index_in_dim(wg, expert, 0, keepdims=False)
        wu_e = lax.dynamic_index_in_dim(wu, expert, 0, keepdims=False)
        wd_e = lax.dynamic_index_in_dim(wd, expert, 0, keepdims=False)
        part_tokens, part_gate, g_gate, g_up, g_down = lax.map(
            lambda w: slice_work(x_sel, dy_sel, p_sel, w[0], w[1], w[2]), (wg_e, wu_e, wd_e))
        tok_sum = jnp.sum(part_tokens.astype(jnp.float32), axis=0)
        gate_sum = jnp.sum(part_gate.astype(jnp.float32), axis=0)
        tok_x = jnp.zeros((block + 1, D), jnp.float32).at[order].add(tok_sum)[:block]
        tok_p = jnp.zeros((block + 1,), jnp.float32).at[order].add(gate_sum)[:block]
        acc_x = acc_x.at[row].add(tok_x)
        acc_p = acc_p.at[row].add(jnp.where(hit, tok_p[:, None], jnp.float32(0.0)))
        acc_g = acc_g.at[expert].add(g_gate.astype(jnp.float32))
        acc_u = acc_u.at[expert].add(g_up.astype(jnp.float32))
        acc_d = acc_d.at[expert].add(g_down.astype(jnp.float32))
        return acc_x, acc_p, acc_g, acc_u, acc_d

    init = (jnp.zeros((N_DP, block, D), jnp.float32),
            jnp.zeros((N_DP, block, TOP), jnp.float32),
            jnp.zeros((EXPERTS, group, D, ffh), jnp.float32),
            jnp.zeros((EXPERTS, group, D, ffh), jnp.float32),
            jnp.zeros((EXPERTS, group, D, ffh), jnp.float32))
    acc_x, acc_p, acc_g, acc_u, acc_d = lax.fori_loop(0, EXPERTS * N_DP, step, init)
    return (acc_x.reshape(TOKENS, D).astype(jnp.bfloat16),
            acc_p.reshape(TOKENS, TOP),
            acc_g.reshape(N_EXPERT, D, ffh).astype(jnp.bfloat16),
            acc_u.reshape(N_EXPERT, D, ffh).astype(jnp.bfloat16),
            acc_d.reshape(N_EXPERT, D, ffh).astype(jnp.bfloat16))
```

```python
import jax
import jax.numpy as jnp
from jax import lax
from jax.sharding import PartitionSpec as P

NY = 4
NZ = 16
Z_GROUPS = [[y * NZ + z for z in range(NZ)] for y in range(NY)]
Y_GROUPS = [[y * NZ + z for y in range(NY)] for z in range(NZ)]


def mult(left, right, dims):
    return lax.dot_general(left, right, (dims, ((), ())), preferred_element_type=jnp.float32)


def shards(tokens, cotangent, expert_ids, gates, w_gate, w_up, w_down_t):
    bf = jnp.bfloat16
    half = lax.rem(lax.axis_index("expert"), NZ) // (NZ // 2)
    experts = jnp.arange(2 * NY, dtype=jnp.int32)
    hit = expert_ids[:, :, None] == experts[None, None, :]
    gate_mat = jnp.sum(jnp.where(hit, gates.astype(jnp.float32)[:, :, None], 0.0), axis=1).astype(bf)
    x = lax.all_gather(tokens, "expert", axis=0, tiled=True, axis_index_groups=Z_GROUPS)
    dy = lax.all_gather(cotangent, "expert", axis=0, tiled=True, axis_index_groups=Z_GROUPS)
    gm = lax.all_gather(gate_mat, "expert", axis=0, tiled=True, axis_index_groups=Z_GROUPS)
    w = jnp.concatenate([w_gate[0], w_up[0], w_down_t[0]], axis=1)
    w = lax.all_gather(w, "dp", axis=0, tiled=True)
    w = lax.all_gather(w, "expert", axis=0, tiled=False, axis_index_groups=Y_GROUPS)
    mine = jnp.where(half == 0, gm[:, 0::2], gm[:, 1::2]).astype(jnp.float32)
    total = 0.0
    parts = []
    grads = []
    for e in range(NY):
        pre = mult(x, w[e, :, :256], ((1,), (0,)))
        back = mult(dy, w[e, :, 256:], ((1,), (0,)))
        pre_gate, pre_up = pre[:, :128], pre[:, 128:]
        weight = mine[:, e : e + 1]
        sig = jax.nn.sigmoid(pre_gate)
        silu = pre_gate * sig
        hidden = silu * pre_up
        parts.append(jnp.sum(hidden * back, axis=1, keepdims=True))
        d_hidden = weight * back
        d_gate = d_hidden * pre_up * sig * (1.0 + pre_gate * (1.0 - sig))
        joined = jnp.concatenate([d_gate, d_hidden * silu], axis=1).astype(bf)
        total = total + mult(joined, w[e, :, :256], ((1,), (1,)))
        grads.append(
            jnp.concatenate(
                [
                    mult(x, joined, ((0,), (0,))),
                    mult(dy, (weight * hidden).astype(bf), ((0,), (0,))),
                ],
                axis=1,
            ).astype(bf)
        )
    part = jnp.concatenate(parts, axis=1)
    zero = jnp.zeros_like(part)
    part = jnp.where(half == 0, jnp.stack([part, zero], 2), jnp.stack([zero, part], 2)).reshape(-1, 2 * NY)
    grad_tokens = lax.psum_scatter(
        total.astype(bf), "expert", scatter_dimension=0, tiled=True, axis_index_groups=Z_GROUPS
    )
    part = lax.psum_scatter(part, "expert", scatter_dimension=0, tiled=True, axis_index_groups=Z_GROUPS)
    grad_gates = jnp.sum(jnp.where(hit, part[:, None, :], 0.0), axis=2)
    g = jnp.stack(grads)
    g = lax.psum_scatter(g, "expert", scatter_dimension=0, tiled=False, axis_index_groups=Y_GROUPS)
    g = lax.psum_scatter(g, "dp", scatter_dimension=0, tiled=True)
    return (grad_tokens, grad_gates, g[None, :, :128], g[None, :, 128:256], g[None, :, 256:])


def solution(mesh):
    row = P(("dp", "expert"), None)
    wide = P("expert", "dp", None)
    return jax.shard_map(
        shards,
        mesh=mesh,
        in_specs=(row, row, row, row, wide, wide, wide),
        out_specs=(row, row, wide, wide, wide),
        check_vma=False,
    )
```

```python
import jax
import jax.numpy as jnp
from jax import lax
from jax.experimental import pallas as pl
from jax.experimental.pallas import tpu as pltpu
from jax.sharding import PartitionSpec as P

NX, NC, NY, NZ = 4, 2, 4, 16
ROWS = 16
D = 3584
LANES = 128
XW = D + LANES
CH = D // NX
QR = 112
FW = 384
C0 = 2 * CH
C1 = XW - C0
MESH = pl.DeviceIdType.MESH
BF = jnp.bfloat16
F32 = jnp.float32
N_SEM = 192


def dot(left, right, dims=((1,), (0,))):
    return lax.dot_general(left, right, (dims, ((), ())), preferred_element_type=F32)


def wrap(value, size):
    return lax.rem(value + size, size)


def kernel(tok, cot, gm, wg, wu, wd, dx_out, part_out, gg, gu, gd,
           xs, ys, w, xt, yt, joined, g, pair, dxa, dxb, rza, rzb,
           p1rel, p1fin, q1rel, q1fin, rel2, fin2, part_acc, ssem, rsem):
    dp = lax.axis_index("dp")
    ex = lax.axis_index("expert")
    x, c = lax.div(dp, NC), lax.rem(dp, NC)
    y, z = lax.div(ex, NZ), lax.rem(ex, NZ)
    half = lax.div(z, NZ // 2)
    other = 1 - c

    def dev(xx, cc, yy, zz):
        return (xx * NC + cc, yy * NZ + zz)

    x_next = (dev(wrap(x + 1, NX), c, y, z), dev(wrap(x - 1, NX), c, y, z))
    y_next = (dev(x, c, wrap(y + 1, NY), z), dev(x, c, wrap(y - 1, NY), z))
    z_next = (dev(x, c, y, wrap(z + 1, NZ)), dev(x, c, y, wrap(z - 1, NZ)))
    sibling = dev(x, other, y, z)

    barrier = pltpu.get_barrier_semaphore()
    for target in (*x_next, *y_next, *z_next, sibling):
        pl.semaphore_signal(barrier, inc=1, device_id=target, device_id_type=MESH)

    xs[z, :, :D] = tok[...]
    xs[z, :, D:] = gm[...]
    ys[z] = cot[...]
    w[y, x, c, :, :, 0:128] = wg[0].reshape(4, QR, 128)
    w[y, x, c, :, :, 128:256] = wu[0].reshape(4, QR, 128)
    w[y, x, c, :, :, 256:384] = wd[0].reshape(4, QR, 128)
    pl.semaphore_wait(barrier, 7)

    count = [0]
    pending = []

    def alloc(n=1):
        base = count[0]
        count[0] += n
        return base

    def xfer(src, dst, i, target):
        return pltpu.make_async_remote_copy(
            src_ref=src, dst_ref=dst, send_sem=ssem.at[i], recv_sem=rsem.at[i],
            device_id=target, device_id_type=MESH)

    def send(src, dst, i, target):
        copy = xfer(src, dst, i, target)
        copy.start()
        pending.append(copy)

    def recv(dst, i):
        xfer(dst, dst, i, sibling).wait_recv()

    z_sem = {(p, d, k): alloc() for p in (0, 1) for d in (0, 1) for k in range(8)}
    blocks = (xs, ys)

    def z_steps(p, d):
        return 8 if p == d else 7

    def z_block(p, d, k):
        return blocks[p].at[wrap(z - k if d == 0 else z + k, NZ)]

    def z_send(p, d, k):
        ref = z_block(p, d, k)
        send(ref, ref, z_sem[p, d, k], z_next[d])

    def z_step(k):
        for p in (0, 1):
            for d in (0, 1):
                if k <= z_steps(p, d):
                    recv(z_block(p, d, k), z_sem[p, d, k - 1])
                if k < z_steps(p, d):
                    z_send(p, d, k)

    first = (x, y)
    second = (y, x)
    first_next = (x_next, y_next)
    second_next = (y_next, x_next)
    shares = []

    def w_at(s, a, b, core, lo, n):
        if s == 0:
            return w.at[b, a, core, pl.ds(lo, n)]
        return w.at[a, b, core, pl.ds(2 + lo, n)]

    def share(s, a, b, lo=0, n=2):
        i = alloc()
        ref = w_at(s, a, b, c, lo, n)
        send(ref, ref, i, sibling)
        shares.append((w_at(s, a, b, other, lo, n), i))

    def pos(value, shift):
        return wrap(value + shift, 4)

    sem_a = {(s, d): alloc() for s in (0, 1) for d in (0, 1)}
    sem_ar = {(s, d): alloc() for s in (0, 1) for d in (0, 1)}
    sem_b = {(s, d, i): alloc() for s in (0, 1) for d in (0, 1) for i in range(4)}
    sem_br = {(s, d, i): alloc() for s in (0, 1) for d in (0, 1) for i in range(4)}
    SHIFT = (0, -1, 1, 2)

    def w_slot_send(s, i):
        a = pos(first[s], SHIFT[i])
        for d in (0, 1):
            ref = w_at(s, a, second[s], c, 0, 2)
            send(ref, ref, sem_b[s, d, i], second_next[s][d])

    def w_start():
        for s in (0, 1):
            for d in (0, 1):
                ref = w_at(s, first[s], second[s], c, 0, 2)
                send(ref, ref, sem_a[s, d], first_next[s][d])
        for s in (0, 1):
            w_slot_send(s, 0)
            share(s, first[s], second[s])

    def w_first():
        for s in (0, 1):
            for d in (0, 1):
                a = pos(first[s], -1 if d == 0 else 1)
                recv(w_at(s, a, second[s], c, 0, 2), sem_a[s, d])
                ref = w_at(s, a, second[s], c, d, 1)
                send(ref, ref, sem_ar[s, d], first_next[s][d])
        for s in (0, 1):
            w_slot_send(s, 1)
            w_slot_send(s, 2)
            share(s, pos(first[s], -1), second[s])
            share(s, pos(first[s], 1), second[s])

    def w_far():
        for s in (0, 1):
            a = pos(first[s], 2)
            for d in (0, 1):
                recv(w_at(s, a, second[s], c, d, 1), sem_ar[s, d])
            w_slot_send(s, 3)
            share(s, a, second[s])

    def w_slot(i):
        for s in (0, 1):
            a = pos(first[s], SHIFT[i])
            for d in (0, 1):
                b = pos(second[s], -1 if d == 0 else 1)
                recv(w_at(s, a, b, c, 0, 2), sem_b[s, d, i])
                ref = w_at(s, a, b, c, d, 1)
                send(ref, ref, sem_br[s, d, i], second_next[s][d])
                share(s, a, b)

    def w_slot_far(i):
        for s in (0, 1):
            a = pos(first[s], SHIFT[i])
            b = pos(second[s], 2)
            for d in (0, 1):
                recv(w_at(s, a, b, c, d, 1), sem_br[s, d, i])
            share(s, a, b)

    for d in (0, 1):
        z_send(0, d, 0)
    w_start()
    for d in (0, 1):
        z_send(1, d, 0)
    z_step(1)
    w_first()
    z_step(2)
    w_slot(0)
    w_far()
    z_step(3)
    w_slot_far(0)
    w_slot(1)
    z_step(4)
    w_slot_far(1)
    w_slot(2)
    z_step(5)
    w_slot_far(2)
    w_slot(3)
    z_step(6)
    w_slot_far(3)
    z_step(7)
    z_step(8)
    for ref, i in shares:
        recv(ref, i)

    def x_cols(ref, k):
        return ref[:, :, k * CH:(k + 1) * CH].reshape(NZ * ROWS, CH)

    for k in range(NX):
        xt[2 * k:2 * k + 2] = x_cols(xs, k).T.reshape(2, CH // 2, NZ * ROWS)
        yt[2 * k:2 * k + 2] = x_cols(ys, k).T.reshape(2, CH // 2, NZ * ROWS)

    part_acc[...] = jnp.zeros_like(part_acc)
    lane = lax.broadcasted_iota(jnp.int32, (NZ * ROWS, LANES), 1)
    order = tuple(pos(y, shift) for shift in (2, 1, -1, 0))
    pair_sem = alloc(4 * NX)

    def pair_copy(i, e, k):
        return xfer(g.at[e, k, other], pair.at[e, k], pair_sem + NX * i + k, sibling)

    def expert(i):
        e = order[i]
        pre = jnp.zeros((NZ * ROWS, 256), F32)
        back = jnp.zeros((NZ * ROWS, 128), F32)
        for k in range(NX):
            wk = w[e, k].reshape(CH, FW)
            pre = pre + dot(x_cols(xs, k), wk[:, :256])
            back = back + dot(x_cols(ys, k), wk[:, 256:])
        mine = lane == 2 * e + half
        gates = xs[:, :, D:].reshape(NZ * ROWS, LANES).astype(F32)
        weight = jnp.sum(jnp.where(mine, gates, 0.0), axis=1, keepdims=True)
        pre_gate, pre_up = pre[:, :128], pre[:, 128:]
        sig = 1.0 / (1.0 + jnp.exp(-pre_gate))
        silu = pre_gate * sig
        hidden = silu * pre_up
        part = jnp.sum(hidden * back, axis=1, keepdims=True)
        part_acc[...] += jnp.where(mine, part, 0.0)
        d_hidden = weight * back
        d_gate = d_hidden * pre_up * sig * (1.0 + pre_gate * (1.0 - sig))
        joined[i, :, :256] = jnp.concatenate([d_gate, d_hidden * silu], axis=1).astype(BF)
        joined[i, :, 256:] = (weight * hidden).astype(BF)

        def grads(k, core):
            row = 2 * k + core
            both = dot(xt[row], joined[i, :, :256])
            down = dot(yt[row], joined[i, :, 256:])
            return jnp.concatenate([both, down], axis=1).reshape(4, QR, FW)

        def away(k, carry):
            g[e, k, other] = grads(k, other).astype(BF)
            pair_copy(i, e, k).start()
            return carry

        def home(k, carry):
            own = grads(k, c)
            pair_copy(i, e, k).wait_recv()
            g[e, k, c] = (own + pair[e, k].astype(F32)).astype(BF)
            return carry

        lax.fori_loop(0, NX, away, 0)
        lax.fori_loop(0, NX, home, 0)

    def add(dst, *sources):
        total = dst[...].astype(F32)
        for source in sources:
            total = total + source[...].astype(F32)
        dst[...] = total.astype(BF)

    p1 = {name: alloc() for name in ("r0", "r1", "f0", "f1")}

    def p1_start():
        for d in (0, 1):
            send(g.at[order[0], :, c, d], p1rel.at[d], p1["r%d" % d], y_next[d])

    def p1_relay(d):
        e = order[1 + d]
        recv(p1rel.at[d], p1["r%d" % d])
        for k in range(NX):
            add(g.at[e, k, c, d], p1rel.at[d, k])
        send(g.at[e, :, c, pl.ds(0, 2)], p1fin.at[d], p1["f%d" % d], y_next[d])

    def p1_end():
        for d in (0, 1):
            recv(p1fin.at[d], p1["f%d" % d])
        for k in range(NX):
            add(g.at[y, k, c, pl.ds(0, 2)], p1fin.at[0, k], p1fin.at[1, k])

    class Ring:
        def __init__(self, at, nexts, relays, finals):
            self.at, self.nexts, self.relays, self.finals = at, nexts, relays, finals
            self.r = [alloc(), alloc()]
            self.f = [alloc(), alloc()]

        def start(self):
            for d in (0, 1):
                send(self.at(2, d, 1), self.relays.at[d], self.r[d], self.nexts[d])

        def relay(self, d):
            shift = 1 if d == 0 else -1
            recv(self.relays.at[d], self.r[d])
            add(self.at(shift, d, 1).at[0], self.relays.at[d, 0])
            send(self.at(shift, 0, 2), self.finals.at[d], self.f[d], self.nexts[d])

        def end(self):
            for d in (0, 1):
                recv(self.finals.at[d], self.f[d])
            add(self.at(0, 0, 2), self.finals.at[0], self.finals.at[1])

    p2 = Ring(lambda sh, lo, n: g.at[y, pos(x, sh), c, pl.ds(lo, n)], x_next, rel2.at[0], fin2.at[0])
    q1 = [
        Ring(lambda sh, lo, n, e=order[i]: g.at[e, pos(x, sh), c, pl.ds(2 + lo, n)], x_next, q1rel.at[i], q1fin.at[i])
        for i in range(NY)
    ]
    q2 = Ring(lambda sh, lo, n: g.at[pos(y, sh), x, c, pl.ds(2 + lo, n)], y_next, rel2.at[1], fin2.at[1])

    def both(ring):
        ring.relay(0)
        ring.relay(1)

    expert(0)
    p1_start()
    q1[0].start()
    expert(1)
    both(q1[0])
    q1[1].start()
    p1_relay(0)
    expert(2)
    q1[2].start()
    p1_relay(1)
    both(q1[1])
    expert(3)
    q1[3].start()

    def token_grads(k):
        total = jnp.zeros((NZ * ROWS, CH), F32)
        for i in range(NY):
            wk = w[order[i], k].reshape(CH, FW)
            total = total + dot(joined[i, :, :256], wk[:, :256], ((1,), (1,)))
        return total.astype(BF).reshape(NZ, ROWS, CH)

    acc = (dxa, dxb)
    land = (rza, rzb)
    back_sem = {(p, d, k): alloc() for p in (0, 1) for d in (0, 1) for k in range(8)}

    def back_target(p, d, k):
        n = z_steps(p, d)
        return wrap(z + n - k if d == 0 else z - n + k, NZ)

    def back_start(p):
        for d in (0, 1):
            send(acc[p].at[back_target(p, d, 0)], land[p].at[d, 0], back_sem[p, d, 0], z_next[d])

    def back_step(k):
        for p in (0, 1):
            for d in (0, 1):
                if k < z_steps(p, d):
                    here = land[p].at[d, k - 1]
                    recv(here, back_sem[p, d, k - 1])
                    add(here, acc[p].at[back_target(p, d, k)])
                    send(here, land[p].at[d, k], back_sem[p, d, k], z_next[d])

    dxa[:, :, :CH] = token_grads(0)
    dxa[:, :, CH:] = token_grads(1)
    back_start(0)
    dxb[:, :, :CH] = token_grads(2)
    dxb[:, :, CH:2 * CH] = token_grads(3)
    dxb[:, :, 2 * CH:] = part_acc[...].astype(BF).reshape(NZ, ROWS, LANES)
    back_start(1)

    q1[0].end()
    q2.start()
    back_step(1)
    both(q1[2])
    q1[1].end()
    q2.relay(0)
    back_step(2)
    p1_end()
    p2.start()
    back_step(3)
    both(q1[3])
    q1[2].end()
    q2.relay(1)
    back_step(4)
    both(p2)
    back_step(5)
    q1[3].end()
    q2.end()
    back_step(6)
    p2.end()
    back_step(7)

    def finish(p):
        total = acc[p][z].astype(F32)
        for d in (0, 1):
            k = z_steps(p, d) - 1
            recv(land[p].at[d, k], back_sem[p, d, k])
            total = total + land[p][d, k].astype(F32)
        return total

    dx_out[:, :C0] = finish(0).astype(BF)
    last = finish(1)
    dx_out[:, C0:] = last[:, :D - C0].astype(BF)
    part_out[...] = last[:, D - C0:]
    for s in (0, 1):
        res = g[y, x, c, 2 * s:2 * s + 2].reshape(2 * QR, FW)
        rows = slice(2 * QR * s, 2 * QR * (s + 1))
        gg[0, rows, :] = res[:, 0:128]
        gu[0, rows, :] = res[:, 128:256]
        gd[0, rows, :] = res[:, 256:384]

    for copy in pending:
        copy.wait_send()

    def drain(i):
        def body(k, carry):
            pair_copy(i, order[i], k).wait_send()
            return carry
        lax.fori_loop(0, NX, body, 0)

    for i in range(NY):
        drain(i)
    assert count[0] <= N_SEM, count[0]


def call(tok, cot, gm, wg, wu, wd):
    vm = pl.BlockSpec(memory_space=pltpu.VMEM)
    out = (
        jax.ShapeDtypeStruct((ROWS, D), BF),
        jax.ShapeDtypeStruct((ROWS, LANES), F32),
        *[jax.ShapeDtypeStruct((1, 448, 128), BF)] * 3,
    )
    scratch = [
        pltpu.VMEM((NZ, ROWS, XW), BF),
        pltpu.VMEM((NZ, ROWS, D), BF),
        pltpu.VMEM((NY, NX, NC, 4, QR, FW), BF),
        pltpu.VMEM((8, 448, 256), BF),
        pltpu.VMEM((8, 448, 256), BF),
        pltpu.VMEM((NY, NZ * ROWS, FW), BF),
        pltpu.VMEM((NY, NX, NC, 4, QR, FW), BF),
        pltpu.VMEM((NY, NX, 4, QR, FW), BF),
        pltpu.VMEM((NZ, ROWS, C0), BF),
        pltpu.VMEM((NZ, ROWS, C1), BF),
        pltpu.VMEM((2, 8, ROWS, C0), BF),
        pltpu.VMEM((2, 8, ROWS, C1), BF),
        pltpu.VMEM((2, NX, QR, FW), BF),
        pltpu.VMEM((2, NX, 2, QR, FW), BF),
        pltpu.VMEM((NY, 2, 1, QR, FW), BF),
        pltpu.VMEM((NY, 2, 2, QR, FW), BF),
        pltpu.VMEM((2, 2, 1, QR, FW), BF),
        pltpu.VMEM((2, 2, 2, QR, FW), BF),
        pltpu.VMEM((NZ * ROWS, LANES), F32),
        pltpu.SemaphoreType.DMA((N_SEM,)),
        pltpu.SemaphoreType.DMA((N_SEM,)),
    ]
    return pl.pallas_call(
        kernel,
        out_shape=out,
        in_specs=[vm] * 6,
        out_specs=(vm,) * 5,
        scratch_shapes=scratch,
        compiler_params=pltpu.CompilerParams(
            collective_id=0, has_side_effects=True, vmem_limit_bytes=60 * 1024 * 1024),
        cost_estimate=pl.CostEstimate(flops=7_600_000_000, bytes_accessed=2_000_000, transcendentals=131072),
    )(tok, cot, gm, wg, wu, wd)


def shards(tokens, cotangent, expert_ids, gates, w_gate, w_up, w_down_t):
    slots = jnp.arange(LANES, dtype=jnp.int32)
    hit = expert_ids[:, :, None] == slots[None, None, :]
    gm = jnp.sum(jnp.where(hit, gates.astype(F32)[:, :, None], 0.0), axis=1).astype(BF)
    grad_tokens, part, gg, gu, gd = call(tokens, cotangent, gm, w_gate, w_up, w_down_t)
    grad_gates = jnp.sum(jnp.where(hit, part[:, None, :], 0.0), axis=2)
    return grad_tokens, grad_gates, gg, gu, gd


def solution(mesh):
    row = P(("dp", "expert"), None)
    wide = P("expert", "dp", None)
    return jax.shard_map(
        shards,
        mesh=mesh,
        in_specs=(row, row, row, row, wide, wide, wide),
        out_specs=(row, row, wide, wide, wide),
        check_vma=False,
    )
```

```python
import jax
import jax.numpy as jnp
from jax import lax
from jax.experimental import pallas as pl
from jax.experimental.pallas import tpu as pltpu
from jax.sharding import PartitionSpec as P

NX, NC, NY, NZ = 4, 2, 4, 16
ROWS = 16
PAIR = NC * ROWS
D = 3584
LANES = 128
DH = D // NC
XW = DH + LANES
PIECE = DH // NX
TOK = NZ * PAIR
CHUNKS = ((0, 8), (8, 4), (12, 4))
PARTS = ((0, 0, 1024), (0, 1024, 896), (1, 0, 896), (1, 896, 896))
HOME = ((0, 896), (896, 1024))
QR = 112
FW = 384
TILE = 256
MESH = pl.DeviceIdType.MESH
BF = jnp.bfloat16
F32 = jnp.float32
N_SEM = 320

ORDER = (
    ("fy", 0), ("fx", 0), ("el", 2, 1), ("el", 3, 1), ("fx", 2), ("fx", 3), ("ty",), ("tx",), ("fx", 1), ("fy", 2),
    ("el", 0, 2), ("dw", 0), ("q10", "s"), ("p10", "s"), ("p12", "s"), ("p11", "s"), ("el", 1, 2), ("dw", 1),
    ("q11", "s"), ("el", 2, 2), ("dw", 2), ("p10", "r", 1), ("q12", "s"), ("p10", "r", 0), ("q10", "r", 0),
    ("p12", "r", 1), ("q11", "r", 1), ("p12", "r", 0), ("q11", "r", 0), ("q10", "r", 1), ("el", 3, 2), ("dx", 1),
    ("hs", 1), ("p11", "r", 1), ("dx", 0), ("hs", 0), ("dw", 3), ("h", 1, 1, 1, 1), ("h", 1, 0, 0, 1),
    ("h", 0, 1, 0, 1), ("h", 0, 1, 1, 1), ("q13", "s"), ("h", 1, 1, 0, 1), ("h", 1, 0, 1, 1), ("p10", "e"),
    ("p2", "s"), ("h", 0, 0, 0, 1), ("p11", "r", 0), ("h", 1, 1, 1, 2), ("h", 0, 0, 1, 1), ("h", 1, 0, 0, 2),
    ("q12", "r", 0), ("h", 0, 1, 1, 2), ("h", 0, 1, 0, 2), ("p13", "s"), ("q12", "r", 1), ("h", 1, 0, 1, 2),
    ("h", 1, 1, 0, 2), ("h", 1, 1, 1, 3), ("p12", "e"), ("h", 0, 0, 0, 2), ("h", 0, 0, 1, 2), ("q11", "e"),
    ("h", 1, 0, 0, 3), ("h", 0, 1, 1, 3), ("q10", "e"), ("h", 0, 1, 0, 3), ("h", 1, 0, 1, 3), ("h", 1, 1, 0, 3),
    ("q2", "s"), ("q13", "r", 0), ("q13", "r", 1), ("h", 1, 1, 1, 4), ("h", 0, 0, 1, 3), ("h", 0, 0, 0, 3),
    ("h", 1, 0, 0, 4), ("p11", "e"), ("h", 0, 1, 1, 4), ("h", 0, 1, 0, 4), ("p2", "r", 1), ("h", 1, 0, 1, 4),
    ("p2", "r", 0), ("h", 1, 1, 1, 5), ("h", 0, 0, 0, 4), ("h", 1, 1, 0, 4), ("p13", "r", 0), ("h", 0, 0, 1, 4),
    ("p13", "r", 1), ("h", 1, 0, 0, 5), ("h", 0, 1, 1, 5), ("h", 0, 1, 0, 5), ("h", 1, 0, 1, 5), ("h", 0, 0, 0, 5),
    ("q2", "r", 0), ("h", 1, 1, 1, 6), ("h", 1, 1, 0, 5), ("q12", "e"), ("q2", "r", 1), ("h", 1, 0, 0, 6),
    ("h", 0, 0, 1, 5), ("h", 0, 1, 1, 6), ("h", 0, 1, 0, 6), ("h", 1, 0, 1, 6), ("h", 0, 0, 0, 6),
    ("h", 1, 1, 1, 7), ("h", 1, 1, 0, 6), ("h", 0, 0, 1, 6), ("h", 1, 0, 0, 7), ("p13", "e"), ("h", 0, 1, 1, 7),
    ("q13", "e"), ("h", 0, 0, 0, 7), ("l1",), ("l0",), ("q2", "e"), ("p2", "e"),
)


def dot(left, right, dims=((1,), (0,))):
    return lax.dot_general(left, right, (dims, ((), ())), preferred_element_type=F32)


def wrap(value, size):
    return lax.rem(value + size, size)


def kernel(tok, cot, ids, gates, wg, wu, wd, dx_out, part_out, gw,
           xs, ys, stage, w, xt, yt, pre_s, pre_r, back_s, back_r, joined, g, dxs, land,
           q1rel, q1fin, p1rel, p1fin, rel2, fin2, part_acc, fin, leave, ssem, rsem):
    dp = lax.axis_index("dp")
    ex = lax.axis_index("expert")
    x, c = lax.div(dp, NC), lax.rem(dp, NC)
    y, z = lax.div(ex, NZ), lax.rem(ex, NZ)
    half = lax.div(z, NZ // 2)
    other = 1 - c

    def dev(xx, cc, yy, zz):
        return (xx * NC + cc, yy * NZ + zz)

    x_next = (dev(wrap(x + 1, NX), c, y, z), dev(wrap(x - 1, NX), c, y, z))
    y_next = (dev(x, c, wrap(y + 1, NY), z), dev(x, c, wrap(y - 1, NY), z))
    z_next = (dev(x, c, y, wrap(z + 1, NZ)), dev(x, c, y, wrap(z - 1, NZ)))
    sibling = dev(x, other, y, z)

    barrier = pltpu.get_barrier_semaphore()
    for target in (*x_next, *y_next, *z_next, sibling):
        pl.semaphore_signal(barrier, inc=1, device_id=target, device_id_type=MESH)

    count = [0]
    pending = []

    def alloc(n=1):
        base = count[0]
        count[0] += n
        return base

    def xfer(src, dst, i, target):
        return pltpu.make_async_remote_copy(
            src_ref=src, dst_ref=dst, send_sem=ssem.at[i], recv_sem=rsem.at[i],
            device_id=target, device_id_type=MESH)

    def send(src, dst, i, target):
        copy = xfer(src, dst, i, target)
        copy.start()
        pending.append(copy)

    def recv(dst, i):
        xfer(dst, dst, i, sibling).wait_recv()

    own = pl.ds(pl.multiple_of(c * ROWS, ROWS), ROWS)
    sib = pl.ds(pl.multiple_of(other * ROWS, ROWS), ROWS)
    row_of = (own, sib)

    def split(ref):
        value = ref[...].astype(F32)
        return [
            jnp.concatenate([value[:, PIECE * (2 * k + h):PIECE * (2 * k + h + 1)] for k in range(NX)], axis=1)
            for h in range(NC)
        ]

    w[y, x, :, :, 0:128] = wg[0].reshape(4, QR, 128)
    w[y, x, :, :, 128:256] = wu[0].reshape(4, QR, 128)
    w[y, x, :, :, 256:384] = wd[0].reshape(4, QR, 128)
    slot_ids = lax.broadcasted_iota(jnp.int32, (LANES, ROWS), 0)
    hits = [slot_ids == ids[k:k + 1, :] for k in range(2)]
    gates_t = gates[...].astype(F32)
    gate_mat = sum(jnp.where(hits[k], gates_t[k:k + 1, :], 0.0) for k in range(2)).T.astype(BF)
    for n, (src, dst) in enumerate(((tok, xs), (cot, ys))):
        low, high = split(src)
        dst[0, own, :DH] = jnp.where(c == 0, low, high).astype(BF)
        stage[n] = jnp.where(c == 0, high, low).astype(BF)
    xs[0, own, DH:] = gate_mat
    pl.semaphore_wait(barrier, 7)

    arrays = (xs, ys)
    z_sem = {(n, p, d, k): alloc() for n in range(len(PARTS)) for p in (0, 1) for d in (0, 1) for k in range(8)}
    stage_sem = [alloc(), alloc()]
    gate_sem = [alloc() for _ in CHUNKS]

    def z_steps(p, d):
        return 8 if p == d else 7

    def slot(d, k):
        if k in (0, 8):
            return 0 if k == 0 else NZ - 1
        return 2 * k - 1 + d

    def z_ref(n, p, d, k):
        a, lo, size = PARTS[n]
        size = min(size, DH - lo) if p == 1 else size
        return arrays[a].at[slot(d, k), row_of[p], pl.ds(lo, size)]

    def z_send(n, p, d, k):
        send(z_ref(n, p, d, k), z_ref(n, p, d, k + 1), z_sem[n, p, d, k], z_next[d])

    def stage_send(n):
        if n == 0:
            send(stage.at[0], xs.at[0, own, pl.ds(0, DH)], stage_sem[0], sibling)
        else:
            send(stage.at[1], ys.at[0, own], stage_sem[1], sibling)

    def stage_recv(n):
        recv(arrays[n].at[0, sib, pl.ds(0, DH)], stage_sem[n])

    def gate_part(h, which):
        lo, n = CHUNKS[h]
        return xs.at[lo:lo + n, which, pl.ds(DH, LANES)]

    def gate_share(h):
        send(gate_part(h, own), gate_part(h, own), gate_sem[h], sibling)

    def gate_recv(h):
        recv(gate_part(h, sib), gate_sem[h])

    def z_begin(p, a):
        for n in range(len(PARTS)):
            if PARTS[n][0] == a:
                for d in (0, 1):
                    z_send(n, p, d, 0)

    def z_one(n, p, k):
        for d in (0, 1):
            if k <= z_steps(p, d):
                recv(z_ref(n, p, d, k), z_sem[n, p, d, k - 1])
            if k < z_steps(p, d):
                z_send(n, p, d, k)

    def z_step(k, between=()):
        jobs = list(between)
        for p in (0, 1):
            for n in range(len(PARTS)):
                z_one(n, p, k)
                if jobs:
                    jobs.pop(0)()
        for job in jobs:
            job()

    first = (x, y)
    second = (y, x)
    first_next = (x_next, y_next)
    second_next = (y_next, x_next)

    def w_at(s, a, b, lo, n):
        if s == 0:
            return w.at[b, a, pl.ds(lo, n)]
        return w.at[a, b, pl.ds(2 + lo, n)]

    def pos(value, shift):
        return wrap(value + shift, 4)

    sem_a = {(s, d): alloc() for s in (0, 1) for d in (0, 1)}
    sem_ar = {(s, d): alloc() for s in (0, 1) for d in (0, 1)}
    sem_b = {(s, d, i): alloc() for s in (0, 1) for d in (0, 1) for i in range(4)}
    sem_br = {(s, d, i): alloc() for s in (0, 1) for d in (0, 1) for i in range(4)}
    SHIFT = (0, -1, 1, 2)

    def w_slot_send(s, i):
        a = pos(first[s], SHIFT[i])
        for d in (0, 1):
            ref = w_at(s, a, second[s], 0, 2)
            send(ref, ref, sem_b[s, d, i], second_next[s][d])

    def w_start():
        for s in (0, 1):
            for d in (0, 1):
                ref = w_at(s, first[s], second[s], 0, 2)
                send(ref, ref, sem_a[s, d], first_next[s][d])
        for s in (0, 1):
            w_slot_send(s, 0)

    def w_first():
        for s in (0, 1):
            for d in (0, 1):
                a = pos(first[s], -1 if d == 0 else 1)
                recv(w_at(s, a, second[s], 0, 2), sem_a[s, d])
                ref = w_at(s, a, second[s], d, 1)
                send(ref, ref, sem_ar[s, d], first_next[s][d])
        for s in (0, 1):
            w_slot_send(s, 1)
            w_slot_send(s, 2)

    def w_far():
        for s in (0, 1):
            a = pos(first[s], 2)
            for d in (0, 1):
                recv(w_at(s, a, second[s], d, 1), sem_ar[s, d])
            w_slot_send(s, 3)

    def w_slot(i):
        for s in (0, 1):
            a = pos(first[s], SHIFT[i])
            for d in (0, 1):
                b = pos(second[s], -1 if d == 0 else 1)
                recv(w_at(s, a, b, 0, 2), sem_b[s, d, i])
                ref = w_at(s, a, b, d, 1)
                send(ref, ref, sem_br[s, d, i], second_next[s][d])

    def w_slot_far(i):
        for s in (0, 1):
            a = pos(first[s], SHIFT[i])
            b = pos(second[s], 2)
            for d in (0, 1):
                recv(w_at(s, a, b, d, 1), sem_br[s, d, i])

    order = tuple(pos(y, shift) for shift in (2, 1, -1, 0))
    pre_sem = {(i, h): alloc() for i in range(NY) for h in range(len(CHUNKS))}
    back_sem = {(i, h): alloc() for i in (0, 2) for h in range(len(CHUNKS))}

    def rows(ref, h, lanes):
        lo, n = CHUNKS[h]
        return ref[lo:lo + n, :, lanes].reshape(n * PAIR, -1)

    def span(h):
        lo, n = CHUNKS[h]
        return pl.ds(PAIR * lo, PAIR * n)

    def weights(i, lanes):
        return w[order[i], :, :, :, lanes].reshape(DH, -1)

    def transpose(src, dst, h):
        lo, n = CHUNKS[h]

        def body(j, carry):
            at = pl.ds(pl.multiple_of(j * TILE, TILE), TILE)
            dst[at, span(h)] = src[lo:lo + n, :, at].reshape(n * PAIR, TILE).T
            return carry
        lax.fori_loop(0, DH // TILE, body, 0)

    def pre_copy(i, h):
        return pre_s.at[i, span(h)], pre_r.at[i, span(h)], pre_sem[i, h]

    def back_copy(i, h):
        at = (span(h), pl.ds(128 * i, 256))
        return back_s.at[at], back_r.at[at], back_sem[i, h]

    def fwd_x(i, h):
        pre_s[i, span(h), :] = dot(rows(xs, h, slice(0, DH)), weights(i, slice(0, 256)))
        send(*pre_copy(i, h), sibling)

    def fwd_y(i, h):
        both = jnp.concatenate([weights(i, slice(256, 384)), weights(i + 1, slice(256, 384))], axis=1)
        back_s[span(h), 128 * i:128 * (i + 2)] = dot(rows(ys, h, slice(0, DH)), both)
        send(*back_copy(i, h), sibling)

    def elementwise(i, h):
        e = order[i]
        n = CHUNKS[h][1]
        if i == 0:
            gate_recv(h)
        recv(*pre_copy(i, h)[1:])
        if i % 2 == 0:
            recv(*back_copy(i, h)[1:])
        mine = lax.broadcasted_iota(jnp.int32, (n * PAIR, LANES), 1) == 2 * e + half
        pre = pre_s[i, span(h), :] + pre_r[i, span(h), :]
        back = back_s[span(h), 128 * i:128 * (i + 1)] + back_r[span(h), 128 * i:128 * (i + 1)]
        gate = rows(xs, h, slice(DH, XW)).astype(F32)
        weight = jnp.sum(jnp.where(mine, gate, 0.0), axis=1, keepdims=True)
        pre_gate, pre_up = pre[:, :128], pre[:, 128:]
        sig = 1.0 / (1.0 + jnp.exp(-pre_gate))
        silu = pre_gate * sig
        hidden = silu * pre_up
        part = jnp.where(mine, jnp.sum(hidden * back, axis=1, keepdims=True), 0.0)
        part_acc[span(h), :] = part if i == 0 else part_acc[span(h), :] + part
        d_hidden = weight * back
        d_gate = d_hidden * pre_up * sig * (1.0 + pre_gate * (1.0 - sig))
        joined[i, span(h), 0:128] = d_gate.astype(BF)
        joined[i, span(h), 128:256] = (d_hidden * silu).astype(BF)
        joined[i, span(h), 256:384] = (weight * hidden).astype(BF)

    def weight_grads(i):
        e = order[i]

        def body(k, carry):
            at = pl.ds(pl.multiple_of(k * PIECE, PIECE), PIECE)
            g[e, k, :, :, 0:256] = dot(xt[at, :], joined[i, :, 0:256]).astype(BF).reshape(4, QR, 256)
            g[e, k, :, :, 256:384] = dot(yt[at, :], joined[i, :, 256:384]).astype(BF).reshape(4, QR, 128)
            return carry
        lax.fori_loop(0, NX, body, 0)

    def token_grads(k, lo):
        at = pl.ds(lo * PAIR, NZ // 2 * PAIR)
        total = jnp.zeros((NZ // 2 * PAIR, DH // 2), F32)
        for i in range(NY):
            wk = w[order[i], 2 * k:2 * k + 2, :, :, 0:256].reshape(DH // 2, 256)
            total = total + dot(joined[i, at, 0:256], wk, ((1,), (1,)))
        dxs[lo:lo + NZ // 2, :, k * (DH // 2):(k + 1) * (DH // 2)] = (
            total.astype(BF).reshape(NZ // 2, PAIR, DH // 2))
        if k == 1:
            dxs[lo:lo + NZ // 2, :, DH:] = part_acc[at, :].astype(BF).reshape(NZ // 2, PAIR, LANES)

    def later(fn, *args):
        return lambda: fn(*args)

    stage_send(0)
    z_begin(0, 0)
    w_start()
    stage_send(1)
    z_begin(0, 1)
    stage_recv(0)
    z_begin(1, 0)
    stage_recv(1)
    z_begin(1, 1)
    w_first()
    z_step(1)
    w_slot(0)
    w_far()
    z_step(2)
    w_slot(1)
    z_step(3)
    w_slot(2)
    w_slot_far(0)
    z_step(4)
    w_slot(3)
    w_slot_far(1)
    gate_share(0)
    z_step(5, [later(transpose, xs, xt, 0), later(transpose, ys, yt, 0)])
    w_slot_far(2)
    w_slot_far(3)
    z_step(6, [later(fwd_x, i, 0) for i in range(NY)] + [later(fwd_y, 0, 0), later(fwd_y, 2, 0)])
    gate_share(1)
    z_step(7, [job for i in range(NY) for job in (later(elementwise, i, 0), later(fwd_x, i, 1))])
    z_step(8, [
        later(fwd_y, 0, 1), later(fwd_y, 2, 1), later(transpose, xs, xt, 1), later(transpose, ys, yt, 1),
        later(token_grads, 0, 0), later(token_grads, 1, 0), later(elementwise, 0, 1), later(elementwise, 1, 1)])
    gate_share(2)

    def add(dst, *sources):
        total = dst[...].astype(F32)
        for source in sources:
            total = total + source[...].astype(F32)
        dst[...] = total.astype(BF)

    class Ring:
        def __init__(self, at, nexts, relays, finals):
            self.at, self.nexts, self.relays, self.finals = at, nexts, relays, finals
            self.r = [alloc(), alloc()]
            self.f = [alloc(), alloc()]

        def start(self):
            for d in (0, 1):
                send(self.at(2, d, 1), self.relays.at[d], self.r[d], self.nexts[d])

        def relay(self, d):
            shift = 1 if d == 0 else -1
            recv(self.relays.at[d], self.r[d])
            add(self.at(shift, d, 1), self.relays.at[d])
            send(self.at(shift, 0, 2), self.finals.at[d], self.f[d], self.nexts[d])

        def end(self):
            for d in (0, 1):
                recv(self.finals.at[d], self.f[d])
            add(self.at(0, 0, 2), self.finals.at[0], self.finals.at[1])

    order_x = tuple(pos(x, shift) for shift in (2, 1, -1, 0))
    p1 = [
        Ring(lambda sh, lo, n, a=order_x[i]: g.at[pos(y, sh), a, pl.ds(lo, n)], y_next, p1rel.at[i], p1fin.at[i])
        for i in range(NX)
    ]
    q1 = [
        Ring(lambda sh, lo, n, e=order[i]: g.at[e, pos(x, sh), pl.ds(2 + lo, n)], x_next, q1rel.at[i], q1fin.at[i])
        for i in range(NY)
    ]
    p2 = Ring(lambda sh, lo, n: g.at[y, pos(x, sh), pl.ds(lo, n)], x_next, rel2.at[0], fin2.at[0])
    q2 = Ring(lambda sh, lo, n: g.at[pos(y, sh), x, pl.ds(2 + lo, n)], y_next, rel2.at[1], fin2.at[1])

    home_sem = {(p, m, d, k): alloc() for p in (0, 1) for m in (0, 1) for d in (0, 1) for k in range(8)}
    fin_sem = alloc()

    def home_lanes(p, m):
        lo, size = HOME[m]
        return pl.ds(lo, min(size, DH - lo) if p == 1 else size)

    def home_src(p, m, d, k):
        return dxs.at[slot(1 - d, z_steps(p, d) - k), row_of[p], home_lanes(p, m)]

    def home_land(p, m, d, k):
        return land.at[p, d, k, :, home_lanes(p, m)]

    def home_start(m):
        for p in (1, 0):
            for d in (0, 1):
                send(home_src(p, m, d, 0), home_land(p, m, d, 0), home_sem[p, m, d, 0], z_next[d])

    def home_step(m, p, d, k):
        here = home_land(p, m, d, k - 1)
        recv(here, home_sem[p, m, d, k - 1])
        add(here, home_src(p, m, d, k))
        send(here, home_land(p, m, d, k), home_sem[p, m, d, k], z_next[d])

    def home_last(p):
        lanes = slice(0, DH if p == 1 else XW)
        total = dxs[0, row_of[p], lanes].astype(F32)
        for d in (0, 1):
            k = z_steps(p, d) - 1
            for m in (0, 1):
                recv(home_land(p, m, d, k), home_sem[p, m, d, k])
            total = total + land[p, d, k, :, lanes].astype(F32)
        return total

    def last_sibling():
        leave[...] = home_last(1).astype(BF)
        send(leave, fin.at[c], fin_sem, sibling)

    def last_own():
        mine = home_last(0)
        fin[c] = mine[:, :DH].astype(BF)
        part = mine[:, DH:].T
        part_out[...] = jnp.concatenate(
            [jnp.sum(jnp.where(hits[k], part, 0.0), axis=0, keepdims=True) for k in range(2)], axis=0)

    jobs = {
        "fx": lambda i: fwd_x(i, 2),
        "fy": lambda i: fwd_y(i, 2),
        "tx": lambda: transpose(xs, xt, 2),
        "ty": lambda: transpose(ys, yt, 2),
        "el": elementwise,
        "dw": weight_grads,
        "dx": lambda m: token_grads(m, NZ // 2),
        "hs": home_start,
        "h": home_step,
        "l1": last_sibling,
        "l0": last_own,
    }
    rings = {"p1%d" % i: ring for i, ring in enumerate(p1)}
    rings.update({"q1%d" % i: ring for i, ring in enumerate(q1)})
    rings.update({"p2": p2, "q2": q2})
    for name, *rest in ORDER:
        if name in rings:
            {"s": rings[name].start, "r": rings[name].relay, "e": rings[name].end}[rest[0]](*rest[1:])
        else:
            jobs[name](*rest)

    gw[...] = g[y, x].reshape(4 * QR, FW)
    recv(fin.at[other], fin_sem)
    low, high = fin[0].astype(F32), fin[1].astype(F32)
    dx_out[...] = jnp.concatenate(
        [part[:, PIECE * k:PIECE * (k + 1)] for k in range(NX) for part in (low, high)], axis=1).astype(BF)

    for copy in pending:
        copy.wait_send()
    assert count[0] <= N_SEM, count[0]


def call(tok, cot, ids, gates, wg, wu, wd):
    vm = pl.BlockSpec(memory_space=pltpu.VMEM)
    out = (
        jax.ShapeDtypeStruct((ROWS, D), BF),
        jax.ShapeDtypeStruct((2, ROWS), F32),
        jax.ShapeDtypeStruct((4 * QR, FW), BF),
    )
    scratch = [
        pltpu.VMEM((NZ, PAIR, XW), BF),
        pltpu.VMEM((NZ, PAIR, DH), BF),
        pltpu.VMEM((2, ROWS, DH), BF),
        pltpu.VMEM((NY, NX, 4, QR, FW), BF),
        pltpu.VMEM((DH, TOK), BF),
        pltpu.VMEM((DH, TOK), BF),
        pltpu.VMEM((NY, TOK, 256), F32),
        pltpu.VMEM((NY, TOK, 256), F32),
        pltpu.VMEM((TOK, 512), F32),
        pltpu.VMEM((TOK, 512), F32),
        pltpu.VMEM((NY, TOK, FW), BF),
        pltpu.VMEM((NY, NX, 4, QR, FW), BF),
        pltpu.VMEM((NZ, PAIR, XW), BF),
        pltpu.VMEM((2, 2, 8, ROWS, XW), BF),
        pltpu.VMEM((NY, 2, 1, QR, FW), BF),
        pltpu.VMEM((NY, 2, 2, QR, FW), BF),
        pltpu.VMEM((NX, 2, 1, QR, FW), BF),
        pltpu.VMEM((NX, 2, 2, QR, FW), BF),
        pltpu.VMEM((2, 2, 1, QR, FW), BF),
        pltpu.VMEM((2, 2, 2, QR, FW), BF),
        pltpu.VMEM((TOK, LANES), F32),
        pltpu.VMEM((NC, ROWS, DH), BF),
        pltpu.VMEM((ROWS, DH), BF),
        pltpu.SemaphoreType.DMA((N_SEM,)),
        pltpu.SemaphoreType.DMA((N_SEM,)),
    ]
    return pl.pallas_call(
        kernel,
        out_shape=out,
        in_specs=[vm] * 7,
        out_specs=(vm,) * 3,
        scratch_shapes=scratch,
        compiler_params=pltpu.CompilerParams(
            collective_id=0, has_side_effects=True, vmem_limit_bytes=60 * 1024 * 1024),
        cost_estimate=pl.CostEstimate(flops=7_600_000_000, bytes_accessed=2_000_000, transcendentals=262144),
    )(tok, cot, ids, gates, wg, wu, wd)


def shards(tokens, cotangent, expert_ids, gates, w_gate, w_up, w_down_t):
    grad_tokens, grad_gates, gw = call(
        tokens, cotangent, expert_ids.T, gates.T, w_gate, w_up, w_down_t)
    return grad_tokens, grad_gates.T, gw[None, :, :128], gw[None, :, 128:256], gw[None, :, 256:]


def solution(mesh):
    row = P(("dp", "expert"), None)
    wide = P("expert", "dp", None)
    return jax.shard_map(
        shards,
        mesh=mesh,
        in_specs=(row, row, row, row, wide, wide, wide),
        out_specs=(row, row, wide, wide, wide),
        check_vma=False,
    )
```

```python
import jax
import jax.numpy as jnp
from jax import lax
from jax.experimental import pallas as pl
from jax.experimental.pallas import tpu as pltpu
from jax.sharding import PartitionSpec as P

NX, NC, NY, NZ = 4, 2, 4, 16
ROWS = 16
PAIR = NC * ROWS
D = 3584
LANES = 128
DH = D // NC
XW = DH + LANES
PIECE = DH // NX
TOK = NZ * PAIR
CHUNKS = ((0, 8), (8, 4), (12, 4))
PARTS = ((0, 0, 1024), (0, 1024, 896), (1, 0, 896), (1, 896, 896))
HOME = ((0, 896), (896, 1024))
QR = 112
FW = 384
TILE = 256
MESH = pl.DeviceIdType.MESH
BF = jnp.bfloat16
F32 = jnp.float32
N_SEM = 352

ORDER = (
    ("fy", 0), ("fx", 0), ("tx",), ("fy", 2), ("fx", 2), ("fx", 3), ("fx", 1), ("el", 0, 1), ("el", 1, 1), ("el", 2, 1), ("el", 3, 1), ("ty",),
    ("el", 0, 2), ("dw", 0), ("p11", "s"), ("p13", "s"), ("q10", "s"), ("q10", "d", 1), ("q10", "d", 0),
    ("p10", "s"), ("p12", "s"), ("el", 1, 2), ("dw", 1), ("p10", "d", 0), ("p12", "d", 0), ("p13", "d", 0),
    ("q11", "s"), ("q11", "d", 0), ("el", 2, 2), ("el", 3, 2), ("dx", 0), ("hs", 0), ("dx", 1), ("hs", 1),
    ("q10", "r", 0), ("q10", "r", 1), ("p13", "r", 0), ("dw", 2), ("h", 0, 1, 0, 1), ("h", 0, 0, 1, 1),
    ("h", 0, 0, 0, 1), ("h", 0, 1, 1, 1), ("h", 1, 1, 0, 1), ("h", 1, 1, 1, 1), ("q11", "r", 0), ("h", 1, 0, 0, 1),
    ("h", 1, 0, 1, 1), ("p10", "d", 1), ("p10", "r", 1), ("p11", "d", 1), ("p11", "r", 1), ("q12", "s"),
    ("p12", "d", 1), ("p12", "r", 1), ("p13", "d", 1), ("p12", "r", 0), ("h", 0, 0, 1, 2), ("p10", "r", 0),
    ("h", 0, 0, 0, 2), ("h", 0, 1, 1, 2), ("q12", "d", 1), ("p11", "d", 0), ("h", 1, 1, 0, 2), ("h", 1, 1, 1, 2),
    ("p11", "r", 0), ("h", 1, 0, 0, 2), ("h", 1, 0, 1, 2), ("h", 0, 1, 0, 2), ("q12", "d", 0), ("p13", "r", 1),
    ("q11", "d", 1), ("q11", "r", 1), ("q10", "e"), ("q2", "s"), ("h", 0, 0, 1, 3), ("h", 0, 0, 0, 3),
    ("h", 0, 1, 1, 3), ("q12", "r", 0), ("h", 1, 1, 1, 3), ("h", 1, 1, 0, 3), ("q12", "r", 1), ("h", 1, 0, 0, 3),
    ("h", 1, 0, 1, 3), ("dw", 3), ("h", 0, 1, 0, 3), ("h", 0, 1, 1, 4), ("h", 0, 0, 0, 4), ("h", 1, 1, 0, 4),
    ("h", 1, 1, 1, 4), ("q13", "s"), ("q13", "d", 0), ("q13", "d", 1), ("h", 1, 0, 0, 4), ("h", 1, 0, 1, 4),
    ("p10", "e"), ("p2", "s"), ("h", 0, 0, 1, 4), ("q11", "e"), ("q2", "d", 0), ("h", 0, 1, 0, 4),
    ("h", 0, 1, 1, 5), ("q12", "e"), ("h", 1, 1, 1, 5), ("h", 0, 0, 0, 5), ("q2", "d", 1), ("p12", "e"),
    ("h", 1, 0, 1, 5), ("h", 1, 0, 0, 5), ("p11", "e"), ("h", 0, 0, 1, 5), ("q13", "r", 1), ("p2", "d", 0),
    ("h", 1, 1, 0, 5), ("h", 0, 1, 1, 6), ("p2", "d", 1), ("h", 0, 1, 0, 5), ("q2", "r", 0), ("h", 1, 1, 1, 6),
    ("h", 0, 0, 0, 6), ("q13", "r", 0), ("p13", "e"), ("h", 1, 0, 0, 6), ("h", 1, 0, 1, 6), ("p2", "r", 1),
    ("h", 0, 0, 1, 6), ("p2", "r", 0), ("h", 1, 1, 0, 6), ("h", 0, 1, 1, 7), ("q2", "r", 1), ("h", 0, 1, 0, 6),
    ("h", 1, 1, 1, 7), ("h", 0, 0, 0, 7), ("h", 1, 0, 0, 7), ("q13", "e"), ("l1",), ("p2", "e"), ("q2", "e"),
    ("l0",),
)


def dot(left, right, dims=((1,), (0,))):
    return lax.dot_general(left, right, (dims, ((), ())), preferred_element_type=F32)


def wrap(value, size):
    return lax.rem(value + size, size)


def kernel(tok_hbm, cot_hbm, ids, gates, wg_hbm, wu_hbm, wd_hbm, dx_out, part_out, gw,
           xs, ys, stage, w, xt, yt, pre_s, pre_r, back_s, back_r, joined, g, dxs, land,
           q1rel, q1fin, p1rel, p1fin, rel2, fin2, part_acc, fin, leave, tok, cot, wg, wu, wd, insem, ssem, rsem):
    dp = lax.axis_index("dp")
    ex = lax.axis_index("expert")
    x, c = lax.div(dp, NC), lax.rem(dp, NC)
    y, z = lax.div(ex, NZ), lax.rem(ex, NZ)
    half = lax.div(z, NZ // 2)
    other = 1 - c

    def dev(xx, cc, yy, zz):
        return (xx * NC + cc, yy * NZ + zz)

    x_next = (dev(wrap(x + 1, NX), c, y, z), dev(wrap(x - 1, NX), c, y, z))
    y_next = (dev(x, c, wrap(y + 1, NY), z), dev(x, c, wrap(y - 1, NY), z))
    z_next = (dev(x, c, y, wrap(z + 1, NZ)), dev(x, c, y, wrap(z - 1, NZ)))
    sibling = dev(x, other, y, z)

    loads = [
        pltpu.make_async_copy(src, dst, insem.at[i])
        for i, (src, dst) in enumerate(
            ((wg_hbm, wg), (wu_hbm, wu), (wd_hbm, wd), (tok_hbm, tok), (cot_hbm, cot)))
    ]
    for load in loads:
        load.start()

    barrier = pltpu.get_barrier_semaphore()
    for target in (*x_next, *y_next, *z_next, sibling):
        pl.semaphore_signal(barrier, inc=1, device_id=target, device_id_type=MESH)

    count = [0]
    pending = []

    def alloc(n=1):
        base = count[0]
        count[0] += n
        return base

    def xfer(src, dst, i, target):
        return pltpu.make_async_remote_copy(
            src_ref=src, dst_ref=dst, send_sem=ssem.at[i], recv_sem=rsem.at[i],
            device_id=target, device_id_type=MESH)

    def send(src, dst, i, target):
        copy = xfer(src, dst, i, target)
        copy.start()
        pending.append(copy)

    def recv(dst, i):
        xfer(dst, dst, i, sibling).wait_recv()

    own = pl.ds(pl.multiple_of(c * ROWS, ROWS), ROWS)
    sib = pl.ds(pl.multiple_of(other * ROWS, ROWS), ROWS)
    row_of = (own, sib)

    def split(ref):
        value = ref[...].astype(F32)
        return [
            jnp.concatenate([value[:, PIECE * (2 * k + h):PIECE * (2 * k + h + 1)] for k in range(NX)], axis=1)
            for h in range(NC)
        ]

    for load in loads:
        load.wait()
    w[y, x, :, :, 0:128] = wg[0].reshape(4, QR, 128)
    w[y, x, :, :, 128:256] = wu[0].reshape(4, QR, 128)
    w[y, x, :, :, 256:384] = wd[0].reshape(4, QR, 128)
    slot_ids = lax.broadcasted_iota(jnp.int32, (LANES, ROWS), 0)
    hits = [slot_ids == ids[k:k + 1, :] for k in range(2)]
    gates_t = gates[...].astype(F32)
    gate_mat = sum(jnp.where(hits[k], gates_t[k:k + 1, :], 0.0) for k in range(2)).T.astype(BF)
    for n, (src, dst) in enumerate(((tok, xs), (cot, ys))):
        low, high = split(src)
        dst[0, own, :DH] = jnp.where(c == 0, low, high).astype(BF)
        stage[n] = jnp.where(c == 0, high, low).astype(BF)
    xs[0, own, DH:] = gate_mat
    pl.semaphore_wait(barrier, 7)

    arrays = (xs, ys)
    z_sem = {(n, p, d, k): alloc() for n in range(len(PARTS)) for p in (0, 1) for d in (0, 1) for k in range(8)}
    stage_sem = [alloc(), alloc()]
    gate_sem = [alloc() for _ in CHUNKS]

    def z_steps(p, d):
        return 8 if p == d else 7

    def slot(d, k):
        if k in (0, 8):
            return 0 if k == 0 else NZ - 1
        return 2 * k - 1 + d

    def z_ref(n, p, d, k):
        a, lo, size = PARTS[n]
        size = min(size, DH - lo) if p == 1 else size
        return arrays[a].at[slot(d, k), row_of[p], pl.ds(lo, size)]

    def z_send(n, p, d, k):
        send(z_ref(n, p, d, k), z_ref(n, p, d, k + 1), z_sem[n, p, d, k], z_next[d])

    def stage_send(n):
        if n == 0:
            send(stage.at[0], xs.at[0, own, pl.ds(0, DH)], stage_sem[0], sibling)
        else:
            send(stage.at[1], ys.at[0, own], stage_sem[1], sibling)

    def stage_recv(n):
        recv(arrays[n].at[0, sib, pl.ds(0, DH)], stage_sem[n])

    def gate_part(h, which):
        lo, n = CHUNKS[h]
        return xs.at[lo:lo + n, which, pl.ds(DH, LANES)]

    def gate_share(h):
        send(gate_part(h, own), gate_part(h, own), gate_sem[h], sibling)

    def gate_recv(h):
        recv(gate_part(h, sib), gate_sem[h])

    def z_begin(p, a):
        for n in range(len(PARTS)):
            if PARTS[n][0] == a:
                for d in (0, 1):
                    z_send(n, p, d, 0)

    def z_one(n, p, k):
        for d in (0, 1):
            if k <= z_steps(p, d):
                recv(z_ref(n, p, d, k), z_sem[n, p, d, k - 1])
            if k < z_steps(p, d):
                z_send(n, p, d, k)

    def z_step(k, between=()):
        jobs = list(between)
        turns = [(n, p) for p in (0, 1) for n in range(len(PARTS))]
        for turn, (n, p) in enumerate(turns):
            z_one(n, p, k)
            for _ in range(-(-len(jobs) // (len(turns) - turn))):
                jobs.pop(0)()

    first = (x, y)
    second = (y, x)
    first_next = (x_next, y_next)
    second_next = (y_next, x_next)

    def w_at(s, a, b, lo, n):
        if s == 0:
            return w.at[b, a, pl.ds(lo, n)]
        return w.at[a, b, pl.ds(2 + lo, n)]

    def pos(value, shift):
        return wrap(value + shift, 4)

    sem_a = {(s, d): alloc() for s in (0, 1) for d in (0, 1)}
    sem_ar = {(s, d): alloc() for s in (0, 1) for d in (0, 1)}
    sem_b = {(s, d, i): alloc() for s in (0, 1) for d in (0, 1) for i in range(4)}
    sem_br = {(s, d, i): alloc() for s in (0, 1) for d in (0, 1) for i in range(4)}
    SHIFT = (0, -1, 1, 2)

    def w_slot_send(s, i):
        a = pos(first[s], SHIFT[i])
        for d in (0, 1):
            ref = w_at(s, a, second[s], 0, 2)
            send(ref, ref, sem_b[s, d, i], second_next[s][d])

    def w_start():
        for s in (0, 1):
            for d in (0, 1):
                ref = w_at(s, first[s], second[s], 0, 2)
                send(ref, ref, sem_a[s, d], first_next[s][d])
        for s in (0, 1):
            w_slot_send(s, 0)

    def w_first():
        for s in (0, 1):
            for d in (0, 1):
                a = pos(first[s], -1 if d == 0 else 1)
                recv(w_at(s, a, second[s], 0, 2), sem_a[s, d])
                ref = w_at(s, a, second[s], d, 1)
                send(ref, ref, sem_ar[s, d], first_next[s][d])
        for s in (0, 1):
            w_slot_send(s, 1)
            w_slot_send(s, 2)

    def w_far():
        for s in (0, 1):
            a = pos(first[s], 2)
            for d in (0, 1):
                recv(w_at(s, a, second[s], d, 1), sem_ar[s, d])
            w_slot_send(s, 3)

    def w_slot(i):
        for s in (0, 1):
            a = pos(first[s], SHIFT[i])
            for d in (0, 1):
                b = pos(second[s], -1 if d == 0 else 1)
                recv(w_at(s, a, b, 0, 2), sem_b[s, d, i])
                ref = w_at(s, a, b, d, 1)
                send(ref, ref, sem_br[s, d, i], second_next[s][d])

    def w_slot_far(i):
        for s in (0, 1):
            a = pos(first[s], SHIFT[i])
            b = pos(second[s], 2)
            for d in (0, 1):
                recv(w_at(s, a, b, d, 1), sem_br[s, d, i])

    order = tuple(pos(y, shift) for shift in (2, 1, -1, 0))
    pre_sem = {(i, h): alloc() for i in range(NY) for h in range(len(CHUNKS))}
    back_sem = {(i, h): alloc() for i in (0, 2) for h in range(len(CHUNKS))}

    def rows(ref, h, lanes):
        lo, n = CHUNKS[h]
        return ref[lo:lo + n, :, lanes].reshape(n * PAIR, -1)

    def span(h):
        lo, n = CHUNKS[h]
        return pl.ds(PAIR * lo, PAIR * n)

    def weights(i, lanes):
        return w[order[i], :, :, :, lanes].reshape(DH, -1)

    def transpose(src, dst, h):
        lo, n = CHUNKS[h]

        def body(j, carry):
            at = pl.ds(pl.multiple_of(j * TILE, TILE), TILE)
            dst[at, span(h)] = src[lo:lo + n, :, at].reshape(n * PAIR, TILE).T
            return carry
        lax.fori_loop(0, DH // TILE, body, 0)

    def pre_copy(i, h):
        return pre_s.at[i, span(h)], pre_r.at[i, span(h)], pre_sem[i, h]

    def back_copy(i, h):
        at = (span(h), pl.ds(128 * i, 256))
        return back_s.at[at], back_r.at[at], back_sem[i, h]

    def fwd_x(i, h):
        pre_s[i, span(h), :] = dot(rows(xs, h, slice(0, DH)), weights(i, slice(0, 256)))
        send(*pre_copy(i, h), sibling)

    def fwd_y(i, h):
        both = jnp.concatenate([weights(i, slice(256, 384)), weights(i + 1, slice(256, 384))], axis=1)
        back_s[span(h), 128 * i:128 * (i + 2)] = dot(rows(ys, h, slice(0, DH)), both)
        send(*back_copy(i, h), sibling)

    def elementwise(i, h):
        e = order[i]
        n = CHUNKS[h][1]
        if i == 0:
            gate_recv(h)
        recv(*pre_copy(i, h)[1:])
        if i % 2 == 0:
            recv(*back_copy(i, h)[1:])
        mine = lax.broadcasted_iota(jnp.int32, (n * PAIR, LANES), 1) == 2 * e + half
        pre = pre_s[i, span(h), :] + pre_r[i, span(h), :]
        back = back_s[span(h), 128 * i:128 * (i + 1)] + back_r[span(h), 128 * i:128 * (i + 1)]
        gate = rows(xs, h, slice(DH, XW)).astype(F32)
        weight = jnp.sum(jnp.where(mine, gate, 0.0), axis=1, keepdims=True)
        pre_gate, pre_up = pre[:, :128], pre[:, 128:]
        sig = 1.0 / (1.0 + jnp.exp(-pre_gate))
        silu = pre_gate * sig
        hidden = silu * pre_up
        part = jnp.where(mine, jnp.sum(hidden * back, axis=1, keepdims=True), 0.0)
        part_acc[span(h), :] = part if i == 0 else part_acc[span(h), :] + part
        d_hidden = weight * back
        d_gate = d_hidden * pre_up * sig * (1.0 + pre_gate * (1.0 - sig))
        joined[i, span(h), 0:128] = d_gate.astype(BF)
        joined[i, span(h), 128:256] = (d_hidden * silu).astype(BF)
        joined[i, span(h), 256:384] = (weight * hidden).astype(BF)

    def weight_grads(i):
        e = order[i]

        def body(k, carry):
            at = pl.ds(pl.multiple_of(k * PIECE, PIECE), PIECE)
            g[e, k, :, :, 0:256] = dot(xt[at, :], joined[i, :, 0:256]).astype(BF).reshape(4, QR, 256)
            g[e, k, :, :, 256:384] = dot(yt[at, :], joined[i, :, 256:384]).astype(BF).reshape(4, QR, 128)
            return carry
        lax.fori_loop(0, NX, body, 0)

    def token_grads(k, lo):
        at = pl.ds(lo * PAIR, NZ // 2 * PAIR)
        total = jnp.zeros((NZ // 2 * PAIR, DH // 2), F32)
        for i in range(NY):
            wk = w[order[i], 2 * k:2 * k + 2, :, :, 0:256].reshape(DH // 2, 256)
            total = total + dot(joined[i, at, 0:256], wk, ((1,), (1,)))
        dxs[lo:lo + NZ // 2, :, k * (DH // 2):(k + 1) * (DH // 2)] = (
            total.astype(BF).reshape(NZ // 2, PAIR, DH // 2))
        if k == 1:
            dxs[lo:lo + NZ // 2, :, DH:] = part_acc[at, :].astype(BF).reshape(NZ // 2, PAIR, LANES)

    def later(fn, *args):
        return lambda: fn(*args)

    stage_send(0)
    z_begin(0, 0)
    w_start()
    stage_send(1)
    z_begin(0, 1)
    stage_recv(0)
    z_begin(1, 0)
    stage_recv(1)
    z_begin(1, 1)
    w_first()
    z_step(1)
    w_slot(0)
    w_far()
    z_step(2)
    w_slot(1)
    z_step(3)
    w_slot(2)
    w_slot_far(0)
    z_step(4)
    w_slot(3)
    w_slot_far(1)
    gate_share(0)
    z_step(5, [later(transpose, xs, xt, 0), later(transpose, ys, yt, 0)])
    w_slot_far(2)
    w_slot_far(3)
    z_step(6, [later(fwd_x, i, 0) for i in range(NY)] + [later(fwd_y, 0, 0), later(fwd_y, 2, 0)])
    gate_share(1)
    z_step(7, [job for i in range(NY) for job in (later(elementwise, i, 0), later(fwd_x, i, 1))]
           + [later(transpose, xs, xt, 1), later(transpose, ys, yt, 1)])
    z_step(8, [later(fwd_y, 0, 1), later(fwd_y, 2, 1), later(token_grads, 0, 0), later(token_grads, 1, 0)])
    gate_share(2)

    def add(dst, *sources):
        total = dst[...].astype(F32)
        for source in sources:
            total = total + source[...].astype(F32)
        dst[...] = total.astype(BF)

    class Ring:
        def __init__(self, at, nexts, relays, finals):
            self.at, self.nexts, self.relays, self.finals = at, nexts, relays, finals
            self.r = [alloc(), alloc()]
            self.f = [alloc(), alloc()]
            self.g = [alloc(), alloc()]

        def start(self):
            for d in (0, 1):
                send(self.at(2, d, 1), self.relays.at[d], self.r[d], self.nexts[d])

        def direct(self, d):
            shift = 1 if d == 0 else -1
            send(self.at(shift, 1 - d, 1), self.finals.at[d, pl.ds(1 - d, 1)], self.g[d], self.nexts[d])

        def relay(self, d):
            shift = 1 if d == 0 else -1
            recv(self.relays.at[d], self.r[d])
            add(self.at(shift, d, 1), self.relays.at[d])
            send(self.at(shift, d, 1), self.finals.at[d, pl.ds(d, 1)], self.f[d], self.nexts[d])

        def end(self):
            for d in (0, 1):
                recv(self.finals.at[d, pl.ds(1 - d, 1)], self.g[d])
                recv(self.finals.at[d, pl.ds(d, 1)], self.f[d])
            add(self.at(0, 0, 2), self.finals.at[0], self.finals.at[1])

    order_x = tuple(pos(x, shift) for shift in (2, 1, -1, 0))
    p1 = [
        Ring(lambda sh, lo, n, a=order_x[i]: g.at[pos(y, sh), a, pl.ds(lo, n)], y_next, p1rel.at[i], p1fin.at[i])
        for i in range(NX)
    ]
    q1 = [
        Ring(lambda sh, lo, n, e=order[i]: g.at[e, pos(x, sh), pl.ds(2 + lo, n)], x_next, q1rel.at[i], q1fin.at[i])
        for i in range(NY)
    ]
    p2 = Ring(lambda sh, lo, n: g.at[y, pos(x, sh), pl.ds(lo, n)], x_next, rel2.at[0], fin2.at[0])
    q2 = Ring(lambda sh, lo, n: g.at[pos(y, sh), x, pl.ds(2 + lo, n)], y_next, rel2.at[1], fin2.at[1])

    home_sem = {(p, m, d, k): alloc() for p in (0, 1) for m in (0, 1) for d in (0, 1) for k in range(8)}
    fin_sem = alloc()

    def home_lanes(p, m):
        lo, size = HOME[m]
        return pl.ds(lo, min(size, DH - lo) if p == 1 else size)

    def home_src(p, m, d, k):
        return dxs.at[slot(1 - d, z_steps(p, d) - k), row_of[p], home_lanes(p, m)]

    def home_land(p, m, d, k):
        return land.at[p, d, k, :, home_lanes(p, m)]

    def home_start(m):
        for p in (1, 0):
            for d in (0, 1):
                send(home_src(p, m, d, 0), home_land(p, m, d, 0), home_sem[p, m, d, 0], z_next[d])

    def home_step(m, p, d, k):
        here = home_land(p, m, d, k - 1)
        recv(here, home_sem[p, m, d, k - 1])
        add(here, home_src(p, m, d, k))
        send(here, home_land(p, m, d, k), home_sem[p, m, d, k], z_next[d])

    def home_last(p):
        lanes = slice(0, DH if p == 1 else XW)
        total = dxs[0, row_of[p], lanes].astype(F32)
        for d in (0, 1):
            k = z_steps(p, d) - 1
            for m in (0, 1):
                recv(home_land(p, m, d, k), home_sem[p, m, d, k])
            total = total + land[p, d, k, :, lanes].astype(F32)
        return total

    def last_sibling():
        leave[...] = home_last(1).astype(BF)
        send(leave, fin.at[c], fin_sem, sibling)

    def last_own():
        mine = home_last(0)
        fin[c] = mine[:, :DH].astype(BF)
        part = mine[:, DH:].T
        part_out[...] = jnp.concatenate(
            [jnp.sum(jnp.where(hits[k], part, 0.0), axis=0, keepdims=True) for k in range(2)], axis=0)

    jobs = {
        "fx": lambda i: fwd_x(i, 2),
        "fy": lambda i: fwd_y(i, 2),
        "tx": lambda: transpose(xs, xt, 2),
        "ty": lambda: transpose(ys, yt, 2),
        "el": elementwise,
        "dw": weight_grads,
        "dx": lambda m: token_grads(m, NZ // 2),
        "hs": home_start,
        "h": home_step,
        "l1": last_sibling,
        "l0": last_own,
    }
    rings = {"p1%d" % i: ring for i, ring in enumerate(p1)}
    rings.update({"q1%d" % i: ring for i, ring in enumerate(q1)})
    rings.update({"p2": p2, "q2": q2})
    for name, *rest in ORDER:
        if name in rings:
            ring = rings[name]
            {"s": ring.start, "d": ring.direct, "r": ring.relay, "e": ring.end}[rest[0]](*rest[1:])
        else:
            jobs[name](*rest)

    gw[...] = g[y, x].reshape(4 * QR, FW)
    recv(fin.at[other], fin_sem)
    low, high = fin[0].astype(F32), fin[1].astype(F32)
    dx_out[...] = jnp.concatenate(
        [part[:, PIECE * k:PIECE * (k + 1)] for k in range(NX) for part in (low, high)], axis=1).astype(BF)

    for copy in pending:
        copy.wait_send()
    assert count[0] <= N_SEM, count[0]


def call(tok, cot, ids, gates, wg, wu, wd):
    vm = pl.BlockSpec(memory_space=pltpu.VMEM)
    hbm = pl.BlockSpec(memory_space=pltpu.HBM)
    out = (
        jax.ShapeDtypeStruct((ROWS, D), BF),
        jax.ShapeDtypeStruct((2, ROWS), F32),
        jax.ShapeDtypeStruct((4 * QR, FW), BF),
    )
    scratch = [
        pltpu.VMEM((NZ, PAIR, XW), BF),
        pltpu.VMEM((NZ, PAIR, DH), BF),
        pltpu.VMEM((2, ROWS, DH), BF),
        pltpu.VMEM((NY, NX, 4, QR, FW), BF),
        pltpu.VMEM((DH, TOK), BF),
        pltpu.VMEM((DH, TOK), BF),
        pltpu.VMEM((NY, TOK, 256), F32),
        pltpu.VMEM((NY, TOK, 256), F32),
        pltpu.VMEM((TOK, 512), F32),
        pltpu.VMEM((TOK, 512), F32),
        pltpu.VMEM((NY, TOK, FW), BF),
        pltpu.VMEM((NY, NX, 4, QR, FW), BF),
        pltpu.VMEM((NZ, PAIR, XW), BF),
        pltpu.VMEM((2, 2, 8, ROWS, XW), BF),
        pltpu.VMEM((NY, 2, 1, QR, FW), BF),
        pltpu.VMEM((NY, 2, 2, QR, FW), BF),
        pltpu.VMEM((NX, 2, 1, QR, FW), BF),
        pltpu.VMEM((NX, 2, 2, QR, FW), BF),
        pltpu.VMEM((2, 2, 1, QR, FW), BF),
        pltpu.VMEM((2, 2, 2, QR, FW), BF),
        pltpu.VMEM((TOK, LANES), F32),
        pltpu.VMEM((NC, ROWS, DH), BF),
        pltpu.VMEM((ROWS, DH), BF),
        *[pltpu.VMEM((ROWS, D), BF)] * 2,
        *[pltpu.VMEM((1, 4 * QR, 128), BF)] * 3,
        pltpu.SemaphoreType.DMA((5,)),
        pltpu.SemaphoreType.DMA((N_SEM,)),
        pltpu.SemaphoreType.DMA((N_SEM,)),
    ]
    return pl.pallas_call(
        kernel,
        out_shape=out,
        in_specs=[hbm] * 2 + [vm] * 2 + [hbm] * 3,
        out_specs=(vm,) * 3,
        scratch_shapes=scratch,
        compiler_params=pltpu.CompilerParams(
            collective_id=0, has_side_effects=True, vmem_limit_bytes=60 * 1024 * 1024),
        cost_estimate=pl.CostEstimate(flops=7_600_000_000, bytes_accessed=2_000_000, transcendentals=262144),
    )(tok, cot, ids, gates, wg, wu, wd)


def shards(tokens, cotangent, expert_ids, gates, w_gate, w_up, w_down_t):
    grad_tokens, grad_gates, gw = call(
        tokens, cotangent, expert_ids.T, gates.T, w_gate, w_up, w_down_t)
    return grad_tokens, grad_gates.T, gw[None, :, :128], gw[None, :, 128:256], gw[None, :, 256:]


def solution(mesh):
    row = P(("dp", "expert"), None)
    wide = P("expert", "dp", None)
    return jax.shard_map(
        shards,
        mesh=mesh,
        in_specs=(row, row, row, row, wide, wide, wide),
        out_specs=(row, row, wide, wide, wide),
        check_vma=False,
    )
```

```python
import jax
import jax.numpy as jnp
from jax import lax
from jax.experimental import pallas as pl
from jax.experimental.pallas import tpu as pltpu
from jax.sharding import PartitionSpec as P

NX, NC, NY, NZ = 4, 2, 4, 16
ROWS = 16
PAIR = NC * ROWS
D = 3584
LANES = 128
DH = D // NC
XW = DH + LANES
PIECE = DH // NX
TOK = NZ * PAIR
CHUNKS = ((0, 8), (8, 4), (12, 4))
PARTS = ((0, 0, 1024), (0, 1024, 896), (1, 0, 896), (1, 896, 896))
HOME = ((0, 896), (896, 1024))
QR = 112
FW = 384
TILE = 256
MESH = pl.DeviceIdType.MESH
BF = jnp.bfloat16
F32 = jnp.float32
N_SEM = 352

ORDER = (
    ("fx", 0), ("ty",), ("fy", 0), ("fy", 2), ("fx", 2), ("fx", 3), ("fx", 1), ("el", 0, 1), ("el", 1, 1),
    ("el", 2, 1), ("el", 3, 1), ("tx",), ("el", 0, 2), ("dw", 0), ("el", 1, 2), ("q10", "s"), ("p12", "s"),
    ("q10", "d", 1), ("p11", "s"), ("el", 2, 2), ("el", 3, 2), ("dx", 1), ("q10", "d", 0), ("hs", 1), ("dx", 0),
    ("hs", 0), ("p10", "s"), ("dw", 1), ("q10", "r", 0), ("h", 1, 1, 1, 1), ("p12", "d", 0), ("p12", "r", 0),
    ("q10", "r", 1), ("h", 1, 0, 1, 1), ("p10", "d", 0), ("p11", "d", 0), ("h", 0, 1, 1, 1), ("p11", "r", 0),
    ("h", 1, 1, 0, 1), ("h", 0, 0, 1, 1), ("h", 0, 0, 0, 1), ("q11", "s"), ("q11", "d", 1), ("h", 1, 0, 0, 1),
    ("h", 0, 1, 0, 1), ("p10", "r", 0), ("p13", "s"), ("h", 1, 1, 1, 2), ("q11", "d", 0), ("dw", 2),
    ("h", 1, 1, 0, 2), ("h", 0, 0, 1, 2), ("h", 0, 0, 0, 2), ("h", 0, 1, 1, 2), ("h", 1, 0, 0, 2),
    ("h", 1, 0, 1, 2), ("p12", "d", 1), ("p12", "r", 1), ("q11", "r", 0), ("q11", "r", 1), ("q10", "e"),
    ("q2", "s"), ("q12", "s"), ("h", 0, 1, 0, 2), ("p10", "d", 1), ("p10", "r", 1), ("h", 1, 1, 0, 3),
    ("h", 0, 0, 1, 3), ("h", 1, 1, 1, 3), ("h", 0, 0, 0, 3), ("h", 0, 1, 1, 3), ("q12", "d", 1), ("h", 1, 0, 0, 3),
    ("p11", "d", 1), ("p11", "r", 1), ("h", 1, 0, 1, 3), ("q12", "d", 0), ("dw", 3), ("h", 0, 0, 1, 4),
    ("h", 0, 1, 0, 3), ("h", 1, 1, 1, 4), ("h", 0, 0, 0, 4), ("q13", "s"), ("h", 0, 1, 1, 4), ("q12", "r", 1),
    ("h", 1, 0, 0, 4), ("q13", "d", 0), ("h", 1, 0, 1, 4), ("h", 1, 1, 0, 4), ("q11", "e"), ("p12", "e"),
    ("q13", "d", 1), ("q2", "d", 0), ("p13", "d", 0), ("h", 0, 0, 1, 5), ("h", 0, 1, 0, 4), ("q12", "r", 0),
    ("h", 1, 1, 1, 5), ("h", 0, 0, 0, 5), ("p13", "d", 1), ("p13", "r", 1), ("h", 0, 1, 1, 5), ("h", 1, 0, 0, 5),
    ("h", 1, 0, 1, 5), ("h", 1, 1, 0, 5), ("p10", "e"), ("p2", "s"), ("p2", "d", 1), ("q13", "r", 1),
    ("q13", "r", 0), ("h", 0, 0, 1, 6), ("h", 0, 1, 0, 5), ("q2", "r", 0), ("h", 1, 1, 1, 6), ("h", 0, 0, 0, 6),
    ("p13", "r", 0), ("h", 0, 1, 1, 6), ("h", 1, 0, 0, 6), ("p11", "e"), ("p2", "d", 0), ("h", 1, 0, 1, 6),
    ("q12", "e"), ("h", 1, 1, 0, 6), ("q2", "d", 1), ("q2", "r", 1), ("h", 0, 1, 0, 6), ("p2", "r", 1),
    ("h", 1, 1, 1, 7), ("h", 0, 0, 0, 7), ("p2", "r", 0), ("h", 0, 1, 1, 7), ("h", 1, 0, 0, 7), ("p13", "e"),
    ("q13", "e"), ("l1",), ("l0",), ("p2", "e"), ("q2", "e"),
)


def dot(left, right, dims=((1,), (0,))):
    return lax.dot_general(left, right, (dims, ((), ())), preferred_element_type=F32)


def wrap(value, size):
    return lax.rem(value + size, size)


def kernel(tok_hbm, cot_hbm, ids, gates, wg_hbm, wu_hbm, wd_hbm, dx_out, part_out, gw,
           xs, ys, stage, w, xt, yt, pre_s, pre_r, back_s, back_r, joined, g, dxs, land,
           q1rel, q1fin, p1rel, p1fin, rel2, fin2, part_acc, fin, leave, tok, cot, wg, wu, wd, insem, ssem, rsem):
    dp = lax.axis_index("dp")
    ex = lax.axis_index("expert")
    x, c = lax.div(dp, NC), lax.rem(dp, NC)
    y, z = lax.div(ex, NZ), lax.rem(ex, NZ)
    half = lax.div(z, NZ // 2)
    other = 1 - c

    def dev(xx, cc, yy, zz):
        return (xx * NC + cc, yy * NZ + zz)

    x_next = (dev(wrap(x + 1, NX), c, y, z), dev(wrap(x - 1, NX), c, y, z))
    y_next = (dev(x, c, wrap(y + 1, NY), z), dev(x, c, wrap(y - 1, NY), z))
    z_next = (dev(x, c, y, wrap(z + 1, NZ)), dev(x, c, y, wrap(z - 1, NZ)))
    sibling = dev(x, other, y, z)

    loads = [
        pltpu.make_async_copy(src, dst, insem.at[i])
        for i, (src, dst) in enumerate(
            ((wg_hbm, wg), (wu_hbm, wu), (wd_hbm, wd), (tok_hbm, tok), (cot_hbm, cot)))
    ]
    for load in loads:
        load.start()

    barrier = pltpu.get_barrier_semaphore()
    for target in (*x_next, *y_next, *z_next, sibling):
        pl.semaphore_signal(barrier, inc=1, device_id=target, device_id_type=MESH)

    count = [0]
    pending = []

    def alloc(n=1):
        base = count[0]
        count[0] += n
        return base

    def xfer(src, dst, i, target):
        return pltpu.make_async_remote_copy(
            src_ref=src, dst_ref=dst, send_sem=ssem.at[i], recv_sem=rsem.at[i],
            device_id=target, device_id_type=MESH)

    def send(src, dst, i, target):
        copy = xfer(src, dst, i, target)
        copy.start()
        pending.append(copy)

    def recv(dst, i):
        xfer(dst, dst, i, sibling).wait_recv()

    own = pl.ds(pl.multiple_of(c * ROWS, ROWS), ROWS)
    sib = pl.ds(pl.multiple_of(other * ROWS, ROWS), ROWS)
    row_of = (own, sib)

    def split(ref):
        value = ref[...].astype(F32)
        return [
            jnp.concatenate([value[:, PIECE * (2 * k + h):PIECE * (2 * k + h + 1)] for k in range(NX)], axis=1)
            for h in range(NC)
        ]

    for load in loads:
        load.wait()
    w[y, x, :, :, 0:128] = wg[0].reshape(4, QR, 128)
    w[y, x, :, :, 128:256] = wu[0].reshape(4, QR, 128)
    w[y, x, :, :, 256:384] = wd[0].reshape(4, QR, 128)
    slot_ids = lax.broadcasted_iota(jnp.int32, (LANES, ROWS), 0)
    hits = [slot_ids == ids[k:k + 1, :] for k in range(2)]
    gates_t = gates[...].astype(F32)
    gate_mat = sum(jnp.where(hits[k], gates_t[k:k + 1, :], 0.0) for k in range(2)).T.astype(BF)
    for n, (src, dst) in enumerate(((tok, xs), (cot, ys))):
        low, high = split(src)
        dst[0, own, :DH] = jnp.where(c == 0, low, high).astype(BF)
        stage[n] = jnp.where(c == 0, high, low).astype(BF)
    xs[0, own, DH:] = gate_mat
    pl.semaphore_wait(barrier, 7)

    arrays = (xs, ys)
    z_sem = {(n, p, d, k): alloc() for n in range(len(PARTS)) for p in (0, 1) for d in (0, 1) for k in range(8)}
    stage_sem = [alloc(), alloc()]
    gate_sem = [alloc() for _ in CHUNKS]

    def z_steps(p, d):
        return 8 if p == d else 7

    def slot(d, k):
        if k in (0, 8):
            return 0 if k == 0 else NZ - 1
        return 2 * k - 1 + d

    def z_ref(n, p, d, k):
        a, lo, size = PARTS[n]
        size = min(size, DH - lo) if p == 1 else size
        return arrays[a].at[slot(d, k), row_of[p], pl.ds(lo, size)]

    def z_send(n, p, d, k):
        send(z_ref(n, p, d, k), z_ref(n, p, d, k + 1), z_sem[n, p, d, k], z_next[d])

    def stage_send(n):
        if n == 0:
            send(stage.at[0], xs.at[0, own, pl.ds(0, DH)], stage_sem[0], sibling)
        else:
            send(stage.at[1], ys.at[0, own], stage_sem[1], sibling)

    def stage_recv(n):
        recv(arrays[n].at[0, sib, pl.ds(0, DH)], stage_sem[n])

    def gate_part(h, which):
        lo, n = CHUNKS[h]
        return xs.at[lo:lo + n, which, pl.ds(DH, LANES)]

    def gate_share(h):
        send(gate_part(h, own), gate_part(h, own), gate_sem[h], sibling)

    def gate_recv(h):
        recv(gate_part(h, sib), gate_sem[h])

    def z_begin(p, a):
        for n in range(len(PARTS)):
            if PARTS[n][0] == a:
                for d in (0, 1):
                    z_send(n, p, d, 0)

    def z_one(n, p, k):
        for d in (0, 1):
            if k <= z_steps(p, d):
                recv(z_ref(n, p, d, k), z_sem[n, p, d, k - 1])
            if k < z_steps(p, d):
                z_send(n, p, d, k)

    def z_step(k, between=()):
        jobs = list(between)
        turns = [(n, p) for p in (0, 1) for n in range(len(PARTS))]
        for turn, (n, p) in enumerate(turns):
            z_one(n, p, k)
            for _ in range(-(-len(jobs) // (len(turns) - turn))):
                jobs.pop(0)()

    first = (x, y)
    second = (y, x)
    first_next = (x_next, y_next)
    second_next = (y_next, x_next)

    def w_at(s, a, b, lo, n):
        if s == 0:
            return w.at[b, a, pl.ds(lo, n)]
        return w.at[a, b, pl.ds(2 + lo, n)]

    def pos(value, shift):
        return wrap(value + shift, 4)

    sem_a = {(s, d): alloc() for s in (0, 1) for d in (0, 1)}
    sem_ar = {(s, d): alloc() for s in (0, 1) for d in (0, 1)}
    sem_b = {(s, d, i): alloc() for s in (0, 1) for d in (0, 1) for i in range(4)}
    sem_br = {(s, d, i): alloc() for s in (0, 1) for d in (0, 1) for i in range(4)}
    SHIFT = (0, -1, 1, 2)

    def w_slot_send(s, i):
        a = pos(first[s], SHIFT[i])
        for d in (0, 1):
            ref = w_at(s, a, second[s], 0, 2)
            send(ref, ref, sem_b[s, d, i], second_next[s][d])

    def w_start():
        for s in (0, 1):
            for d in (0, 1):
                ref = w_at(s, first[s], second[s], 0, 2)
                send(ref, ref, sem_a[s, d], first_next[s][d])
        for s in (0, 1):
            w_slot_send(s, 0)

    def w_first():
        for s in (0, 1):
            for d in (0, 1):
                a = pos(first[s], -1 if d == 0 else 1)
                recv(w_at(s, a, second[s], 0, 2), sem_a[s, d])
                ref = w_at(s, a, second[s], d, 1)
                send(ref, ref, sem_ar[s, d], first_next[s][d])
        for s in (0, 1):
            w_slot_send(s, 1)
            w_slot_send(s, 2)

    def w_far():
        for s in (0, 1):
            a = pos(first[s], 2)
            for d in (0, 1):
                recv(w_at(s, a, second[s], d, 1), sem_ar[s, d])
            w_slot_send(s, 3)

    def w_slot(i):
        for s in (0, 1):
            a = pos(first[s], SHIFT[i])
            for d in (0, 1):
                b = pos(second[s], -1 if d == 0 else 1)
                recv(w_at(s, a, b, 0, 2), sem_b[s, d, i])
                ref = w_at(s, a, b, d, 1)
                send(ref, ref, sem_br[s, d, i], second_next[s][d])

    def w_slot_far(i):
        for s in (0, 1):
            a = pos(first[s], SHIFT[i])
            b = pos(second[s], 2)
            for d in (0, 1):
                recv(w_at(s, a, b, d, 1), sem_br[s, d, i])

    order = tuple(pos(y, shift) for shift in (2, 1, -1, 0))
    pre_sem = {(i, h): alloc() for i in range(NY) for h in range(len(CHUNKS))}
    back_sem = {(i, h): alloc() for i in (0, 2) for h in range(len(CHUNKS))}

    def rows(ref, h, lanes):
        lo, n = CHUNKS[h]
        return ref[lo:lo + n, :, lanes].reshape(n * PAIR, -1)

    def span(h):
        lo, n = CHUNKS[h]
        return pl.ds(PAIR * lo, PAIR * n)

    def weights(i, lanes):
        return w[order[i], :, :, :, lanes].reshape(DH, -1)

    def transpose(src, dst, h):
        lo, n = CHUNKS[h]

        def body(j, carry):
            at = pl.ds(pl.multiple_of(j * TILE, TILE), TILE)
            dst[at, span(h)] = src[lo:lo + n, :, at].reshape(n * PAIR, TILE).T
            return carry
        lax.fori_loop(0, DH // TILE, body, 0)

    def pre_copy(i, h):
        return pre_s.at[i, span(h)], pre_r.at[i, span(h)], pre_sem[i, h]

    def back_copy(i, h):
        at = (span(h), pl.ds(128 * i, 256))
        return back_s.at[at], back_r.at[at], back_sem[i, h]

    def fwd_x(i, h):
        pre_s[i, span(h), :] = dot(rows(xs, h, slice(0, DH)), weights(i, slice(0, 256)))
        send(*pre_copy(i, h), sibling)

    def fwd_y(i, h):
        both = jnp.concatenate([weights(i, slice(256, 384)), weights(i + 1, slice(256, 384))], axis=1)
        back_s[span(h), 128 * i:128 * (i + 2)] = dot(rows(ys, h, slice(0, DH)), both)
        send(*back_copy(i, h), sibling)

    def elementwise(i, h):
        e = order[i]
        n = CHUNKS[h][1]
        if i == 0:
            gate_recv(h)
        recv(*pre_copy(i, h)[1:])
        if i % 2 == 0:
            recv(*back_copy(i, h)[1:])
        mine = lax.broadcasted_iota(jnp.int32, (n * PAIR, LANES), 1) == 2 * e + half
        pre = pre_s[i, span(h), :] + pre_r[i, span(h), :]
        back = back_s[span(h), 128 * i:128 * (i + 1)] + back_r[span(h), 128 * i:128 * (i + 1)]
        gate = rows(xs, h, slice(DH, XW)).astype(F32)
        weight = jnp.sum(jnp.where(mine, gate, 0.0), axis=1, keepdims=True)
        pre_gate, pre_up = pre[:, :128], pre[:, 128:]
        sig = 1.0 / (1.0 + jnp.exp(-pre_gate))
        silu = pre_gate * sig
        hidden = silu * pre_up
        part = jnp.where(mine, jnp.sum(hidden * back, axis=1, keepdims=True), 0.0)
        part_acc[span(h), :] = part if i == 0 else part_acc[span(h), :] + part
        d_hidden = weight * back
        d_gate = d_hidden * pre_up * sig * (1.0 + pre_gate * (1.0 - sig))
        joined[i, span(h), 0:128] = d_gate.astype(BF)
        joined[i, span(h), 128:256] = (d_hidden * silu).astype(BF)
        joined[i, span(h), 256:384] = (weight * hidden).astype(BF)

    def weight_grads(i):
        e = order[i]

        def body(k, carry):
            at = pl.ds(pl.multiple_of(k * PIECE, PIECE), PIECE)
            g[e, k, :, :, 0:256] = dot(xt[at, :], joined[i, :, 0:256]).astype(BF).reshape(4, QR, 256)
            g[e, k, :, :, 256:384] = dot(yt[at, :], joined[i, :, 256:384]).astype(BF).reshape(4, QR, 128)
            return carry
        lax.fori_loop(0, NX, body, 0)

    def token_grads(k, lo):
        at = pl.ds(lo * PAIR, NZ // 2 * PAIR)
        total = jnp.zeros((NZ // 2 * PAIR, DH // 2), F32)
        for i in range(NY):
            wk = w[order[i], 2 * k:2 * k + 2, :, :, 0:256].reshape(DH // 2, 256)
            total = total + dot(joined[i, at, 0:256], wk, ((1,), (1,)))
        dxs[lo:lo + NZ // 2, :, k * (DH // 2):(k + 1) * (DH // 2)] = (
            total.astype(BF).reshape(NZ // 2, PAIR, DH // 2))
        if k == 1:
            dxs[lo:lo + NZ // 2, :, DH:] = part_acc[at, :].astype(BF).reshape(NZ // 2, PAIR, LANES)

    def later(fn, *args):
        return lambda: fn(*args)

    stage_send(0)
    z_begin(0, 0)
    w_start()
    stage_send(1)
    z_begin(0, 1)
    stage_recv(0)
    z_begin(1, 0)
    stage_recv(1)
    z_begin(1, 1)
    w_first()
    z_step(1)
    w_slot(0)
    w_far()
    z_step(2)
    w_slot(1)
    z_step(3)
    w_slot(2)
    w_slot_far(0)
    z_step(4)
    w_slot(3)
    w_slot_far(1)
    gate_share(0)
    z_step(5, [later(transpose, xs, xt, 0), later(transpose, ys, yt, 0)])
    w_slot_far(2)
    w_slot_far(3)
    z_step(6, [later(fwd_x, i, 0) for i in range(NY)] + [later(fwd_y, 0, 0), later(fwd_y, 2, 0)])
    gate_share(1)
    z_step(7, [job for i in range(NY) for job in (later(elementwise, i, 0), later(fwd_x, i, 1))]
           + [later(transpose, xs, xt, 1), later(transpose, ys, yt, 1)])
    z_step(8, [later(fwd_y, 0, 1), later(fwd_y, 2, 1), later(token_grads, 0, 0), later(token_grads, 1, 0)])
    gate_share(2)

    def add(dst, *sources):
        total = dst[...].astype(F32)
        for source in sources:
            total = total + source[...].astype(F32)
        dst[...] = total.astype(BF)

    class Ring:
        def __init__(self, at, nexts, relays, finals):
            self.at, self.nexts, self.relays, self.finals = at, nexts, relays, finals
            self.r = [alloc(), alloc()]
            self.f = [alloc(), alloc()]
            self.g = [alloc(), alloc()]

        def start(self):
            for d in (0, 1):
                send(self.at(2, d, 1), self.relays.at[d], self.r[d], self.nexts[d])

        def direct(self, d):
            shift = 1 if d == 0 else -1
            send(self.at(shift, 1 - d, 1), self.finals.at[d, pl.ds(1 - d, 1)], self.g[d], self.nexts[d])

        def relay(self, d):
            shift = 1 if d == 0 else -1
            recv(self.relays.at[d], self.r[d])
            add(self.at(shift, d, 1), self.relays.at[d])
            send(self.at(shift, d, 1), self.finals.at[d, pl.ds(d, 1)], self.f[d], self.nexts[d])

        def end(self):
            for d in (0, 1):
                recv(self.finals.at[d, pl.ds(1 - d, 1)], self.g[d])
                recv(self.finals.at[d, pl.ds(d, 1)], self.f[d])
            add(self.at(0, 0, 2), self.finals.at[0], self.finals.at[1])

    order_x = tuple(pos(x, shift) for shift in (2, 1, -1, 0))
    p1 = [
        Ring(lambda sh, lo, n, a=order_x[i]: g.at[pos(y, sh), a, pl.ds(lo, n)], y_next, p1rel.at[i], p1fin.at[i])
        for i in range(NX)
    ]
    q1 = [
        Ring(lambda sh, lo, n, e=order[i]: g.at[e, pos(x, sh), pl.ds(2 + lo, n)], x_next, q1rel.at[i], q1fin.at[i])
        for i in range(NY)
    ]
    p2 = Ring(lambda sh, lo, n: g.at[y, pos(x, sh), pl.ds(lo, n)], x_next, rel2.at[0], fin2.at[0])
    q2 = Ring(lambda sh, lo, n: g.at[pos(y, sh), x, pl.ds(2 + lo, n)], y_next, rel2.at[1], fin2.at[1])

    home_sem = {(p, m, d, k): alloc() for p in (0, 1) for m in (0, 1) for d in (0, 1) for k in range(8)}
    fin_sem = alloc()

    def home_lanes(p, m):
        lo, size = HOME[m]
        return pl.ds(lo, min(size, DH - lo) if p == 1 else size)

    def home_src(p, m, d, k):
        return dxs.at[slot(1 - d, z_steps(p, d) - k), row_of[p], home_lanes(p, m)]

    def home_land(p, m, d, k):
        return land.at[p, d, k, :, home_lanes(p, m)]

    def home_start(m):
        for p in (1, 0):
            for d in (0, 1):
                send(home_src(p, m, d, 0), home_land(p, m, d, 0), home_sem[p, m, d, 0], z_next[d])

    def home_step(m, p, d, k):
        here = home_land(p, m, d, k - 1)
        recv(here, home_sem[p, m, d, k - 1])
        add(here, home_src(p, m, d, k))
        send(here, home_land(p, m, d, k), home_sem[p, m, d, k], z_next[d])

    def home_last(p):
        lanes = slice(0, DH if p == 1 else XW)
        total = dxs[0, row_of[p], lanes].astype(F32)
        for d in (0, 1):
            k = z_steps(p, d) - 1
            for m in (0, 1):
                recv(home_land(p, m, d, k), home_sem[p, m, d, k])
            total = total + land[p, d, k, :, lanes].astype(F32)
        return total

    def last_sibling():
        leave[...] = home_last(1).astype(BF)
        send(leave, fin.at[c], fin_sem, sibling)

    def last_own():
        mine = home_last(0)
        fin[c] = mine[:, :DH].astype(BF)
        part = mine[:, DH:].T
        part_out[...] = jnp.concatenate(
            [jnp.sum(jnp.where(hits[k], part, 0.0), axis=0, keepdims=True) for k in range(2)], axis=0)

    jobs = {
        "fx": lambda i: fwd_x(i, 2),
        "fy": lambda i: fwd_y(i, 2),
        "tx": lambda: transpose(xs, xt, 2),
        "ty": lambda: transpose(ys, yt, 2),
        "el": elementwise,
        "dw": weight_grads,
        "dx": lambda m: token_grads(m, NZ // 2),
        "hs": home_start,
        "h": home_step,
        "l1": last_sibling,
        "l0": last_own,
    }
    rings = {"p1%d" % i: ring for i, ring in enumerate(p1)}
    rings.update({"q1%d" % i: ring for i, ring in enumerate(q1)})
    rings.update({"p2": p2, "q2": q2})
    for name, *rest in ORDER:
        if name in rings:
            ring = rings[name]
            {"s": ring.start, "d": ring.direct, "r": ring.relay, "e": ring.end}[rest[0]](*rest[1:])
        else:
            jobs[name](*rest)

    gw[...] = g[y, x].reshape(4 * QR, FW)
    recv(fin.at[other], fin_sem)
    low, high = fin[0].astype(F32), fin[1].astype(F32)
    dx_out[...] = jnp.concatenate(
        [part[:, PIECE * k:PIECE * (k + 1)] for k in range(NX) for part in (low, high)], axis=1).astype(BF)

    for copy in pending:
        copy.wait_send()
    assert count[0] <= N_SEM, count[0]


def call(tok, cot, ids, gates, wg, wu, wd):
    vm = pl.BlockSpec(memory_space=pltpu.VMEM)
    hbm = pl.BlockSpec(memory_space=pltpu.HBM)
    out = (
        jax.ShapeDtypeStruct((ROWS, D), BF),
        jax.ShapeDtypeStruct((2, ROWS), F32),
        jax.ShapeDtypeStruct((4 * QR, FW), BF),
    )
    scratch = [
        pltpu.VMEM((NZ, PAIR, XW), BF),
        pltpu.VMEM((NZ, PAIR, DH), BF),
        pltpu.VMEM((2, ROWS, DH), BF),
        pltpu.VMEM((NY, NX, 4, QR, FW), BF),
        pltpu.VMEM((DH, TOK), BF),
        pltpu.VMEM((DH, TOK), BF),
        pltpu.VMEM((NY, TOK, 256), F32),
        pltpu.VMEM((NY, TOK, 256), F32),
        pltpu.VMEM((TOK, 512), F32),
        pltpu.VMEM((TOK, 512), F32),
        pltpu.VMEM((NY, TOK, FW), BF),
        pltpu.VMEM((NY, NX, 4, QR, FW), BF),
        pltpu.VMEM((NZ, PAIR, XW), BF),
        pltpu.VMEM((2, 2, 8, ROWS, XW), BF),
        pltpu.VMEM((NY, 2, 1, QR, FW), BF),
        pltpu.VMEM((NY, 2, 2, QR, FW), BF),
        pltpu.VMEM((NX, 2, 1, QR, FW), BF),
        pltpu.VMEM((NX, 2, 2, QR, FW), BF),
        pltpu.VMEM((2, 2, 1, QR, FW), BF),
        pltpu.VMEM((2, 2, 2, QR, FW), BF),
        pltpu.VMEM((TOK, LANES), F32),
        pltpu.VMEM((NC, ROWS, DH), BF),
        pltpu.VMEM((ROWS, DH), BF),
        *[pltpu.VMEM((ROWS, D), BF)] * 2,
        *[pltpu.VMEM((1, 4 * QR, 128), BF)] * 3,
        pltpu.SemaphoreType.DMA((5,)),
        pltpu.SemaphoreType.DMA((N_SEM,)),
        pltpu.SemaphoreType.DMA((N_SEM,)),
    ]
    return pl.pallas_call(
        kernel,
        out_shape=out,
        in_specs=[hbm] * 2 + [vm] * 2 + [hbm] * 3,
        out_specs=(vm,) * 3,
        scratch_shapes=scratch,
        compiler_params=pltpu.CompilerParams(
            collective_id=0, has_side_effects=True, vmem_limit_bytes=60 * 1024 * 1024),
        cost_estimate=pl.CostEstimate(flops=7_600_000_000, bytes_accessed=2_000_000, transcendentals=262144),
    )(tok, cot, ids, gates, wg, wu, wd)


def shards(tokens, cotangent, expert_ids, gates, w_gate, w_up, w_down_t):
    grad_tokens, grad_gates, gw = call(
        tokens, cotangent, expert_ids.T, gates.T, w_gate, w_up, w_down_t)
    return grad_tokens, grad_gates.T, gw[None, :, :128], gw[None, :, 128:256], gw[None, :, 256:]


def solution(mesh):
    row = P(("dp", "expert"), None)
    wide = P("expert", "dp", None)
    return jax.shard_map(
        shards,
        mesh=mesh,
        in_specs=(row, row, row, row, wide, wide, wide),
        out_specs=(row, row, wide, wide, wide),
        check_vma=False,
    )
```
